32 devices in a mesh: row: 8 (over z, y), col: 4 (over x, core).
Axes of the slice: x: 2, y: 2, z: 4, core: 2. Of those that a mesh axis runs over, the one named last changes fastest.
Arguments:
- features: bfloat16 [8192, 512], P(('col', 'row')), may hold values from -6 to 6
- blocks: bfloat16 [8, 4, 12, 128, 128], P('row', 'col'), may hold values from -0.75 to 0.75
- block_rows: int32 [8, 4, 12], P('row', 'col'), may hold values from 0 to 7, as said below
- block_cols: int32 [8, 4, 12], P('row', 'col'), may hold values from 0 to 15, as said below
- block_count: int32 [8, 4], P('row', 'col'), may hold values from 2 to 12, as said below
- weight: bfloat16 [512, 512], replicated, may hold values from -0.25 to 0.25
- bias_vector: float32 [512], replicated, may hold values from -4 to 4
- upstream: bfloat16 [8192, 512], P(('row', 'col')), may hold values from -6 to 6
Outputs:
- activated: bfloat16 [8192, 512], P(('row', 'col'))
- grad_weight: float32 [512, 512], replicated
- grad_bias: float32 [512], replicated
- grad_features: bfloat16 [8192, 512], P(('col', 'row'))
The draws below stay inside these ranges and needn't reach their ends.
Inputs may be any that keep to these rules, and one draw needn't show every extreme that they name: `block_rows`: the live (block row, block column) pairs of one device are distinct. `block_cols`: paired slot by slot with block_rows. `block_count`: live slots come first; some device has exactly 12 live slots.
All inputs are finite; a program needn't handle non-finite values.
Results may differ from the reference program's by a relative error of at most 0.0061.
Values may be sent and summed in bfloat16 or wider, within the bound.
No kernel may reach another device: no remote copies, remote signals or barrier semaphores. Data moves between devices by JAX's collectives and lax.ppermute only.
A program may use at most 64 MiB of HBM per device.

```python
import jax
import jax.numpy as jnp
from jax import lax

HIDDEN_SIZE = 512
BLOCK = 128
ROW_GROUPS = 8
COL_GROUPS = 4
NODES = 8192
RB = 8
CB = 16
MAXB = 12


def block_pattern(key):
    base_key = jax.random.fold_in(key, 7)
    devices_all = ROW_GROUPS * COL_GROUPS
    band_width = max(1, CB // 8)

    def one_device(dev_key):
        weight_key, noise_key, shift_key = jax.random.split(dev_key, 3)
        row_weights = jax.random.randint(weight_key, (RB,), 1, 9)
        noise = jax.random.randint(noise_key, (RB, CB), 0, 8192)
        shift = jax.random.randint(shift_key, (), 0, CB)
        row_ids = jnp.arange(RB, dtype=jnp.int32)
        col_ids = jnp.arange(CB, dtype=jnp.int32)
        centre = (row_ids * CB // RB + shift) % CB
        offset = jnp.abs(col_ids[None, :] - centre[:, None])
        distance = jnp.minimum(offset, CB - offset)
        nearness = 1 + 7 * (distance <= band_width).astype(jnp.int32)
        scores = noise * row_weights[:, None] * nearness
        scores = scores * (RB * CB) + jnp.arange(RB * CB, dtype=jnp.int32).reshape(RB, CB)
        order = jnp.argsort(-scores.reshape(-1))
        return order[:MAXB].astype(jnp.int32)
    dev_keys = jax.random.split(base_key, devices_all)
    return jax.vmap(one_device)(dev_keys).reshape(ROW_GROUPS, COL_GROUPS, MAXB)


def draw_block_rows(key, part):
    return (block_pattern(key) // CB).astype(jnp.int32)


def draw_block_cols(key, part):
    return (block_pattern(key) % CB).astype(jnp.int32)


def draw_block_count(key, part):
    devices_all = ROW_GROUPS * COL_GROUPS
    divisor = jax.random.randint(jax.random.fold_in(key, 11), (devices_all,), 1, 7)
    counts = jnp.maximum(1, MAXB // divisor)
    fullest = jax.random.randint(jax.random.fold_in(key, 13), (), 0, devices_all)
    counts = counts.at[fullest].set(MAXB)
    return counts.reshape(ROW_GROUPS, COL_GROUPS).astype(jnp.int32)


def level_of(own_key, dims, pieces, low, largest):
    def one(axis_at, shards_of):
        heights = jax.random.uniform(jax.random.fold_in(jax.random.fold_in(own_key, 6), axis_at), (shards_of,), jnp.float32, low / len(pieces), largest / len(pieces))
        return jnp.repeat(jnp.exp(heights), dims[axis_at] // shards_of).reshape((-1,) + (1,) * (len(dims) - axis_at - 1))

    loudness = one(*pieces[0])
    for cut in pieces[1:]:
        loudness = loudness * one(*cut)
    return loudness


def bell_draw(own_key, dims, scale, most, cuts=(), held_as=jnp.bfloat16):
    drawn = scale * jax.random.normal(own_key, dims, jnp.float32)
    if cuts:
        drawn = drawn * level_of(own_key, dims, cuts, -0.22, 0.18)
    return jnp.clip(drawn, -most, most).astype(held_as)


def setup_inputs(seed: int = 0) -> dict:
    splits = jax.random.split(jax.random.key(seed), 9)
    features = bell_draw(splits[0], (NODES, HIDDEN_SIZE), 1.0, 6.0, ((0, 32),))
    blocks = bell_draw(splits[1], (ROW_GROUPS, COL_GROUPS, MAXB, BLOCK, BLOCK), ((BLOCK * MAXB * COL_GROUPS // (2 * RB)) ** -0.5), 0.75, ((0, 8), (1, 4)))
    block_rows = draw_block_rows(jax.random.fold_in(splits[8], 71), 0)
    block_cols = draw_block_cols(jax.random.fold_in(splits[8], 71), 0)
    block_count = draw_block_count(jax.random.fold_in(splits[8], 71), 0)
    weight = bell_draw(splits[5], (HIDDEN_SIZE, HIDDEN_SIZE), HIDDEN_SIZE ** -0.5, 0.25)
    bias_vector = bell_draw(splits[6], (HIDDEN_SIZE,), 1.0, 4.0, (), jnp.float32)
    upstream = bell_draw(splits[7], (NODES, HIDDEN_SIZE), 1.0, 6.0, ((0, 32),))
    return {"features": features, "blocks": blocks, "block_rows": block_rows, "block_cols": block_cols, "block_count": block_count, "weight": weight, "bias_vector": bias_vector, "upstream": upstream}


def reference(features, blocks, block_rows, block_cols, block_count, weight, bias_vector, upstream):
    node_total = features.shape[0]
    width = features.shape[1]
    devices_all = ROW_GROUPS * COL_GROUPS
    block_tiles = blocks.reshape(devices_all, MAXB, BLOCK, BLOCK)
    row_index = jnp.arange(devices_all, dtype=jnp.int32) // COL_GROUPS
    col_index = jnp.arange(devices_all, dtype=jnp.int32) % COL_GROUPS
    row_global = (row_index[:, None] * RB + block_rows.reshape(devices_all, MAXB)).astype(jnp.int32)
    col_global = (col_index[:, None] * CB + block_cols.reshape(devices_all, MAXB)).astype(jnp.int32)
    live_mask = jnp.arange(MAXB, dtype=jnp.int32)[None, :] < block_count.reshape(devices_all, 1)
    zero_blocks = jnp.zeros((node_total // BLOCK, BLOCK, width), jnp.float32)
    feature_blocks = features.reshape(node_total // BLOCK, BLOCK, width)

    def forward_one(totals, device):
        picked = feature_blocks[col_global[device]].astype(jnp.float32)
        chosen = jnp.where(live_mask[device][:, None, None], block_tiles[device], jnp.zeros_like(block_tiles[device])).astype(jnp.float32)
        product = jnp.einsum('sij,sjh->sih', chosen, picked)
        return (totals.at[row_global[device]].add(product), None)
    hidden_sum, unused = lax.scan(forward_one, zero_blocks, jnp.arange(devices_all, dtype=jnp.int32))
    hidden = hidden_sum.reshape(node_total, width).astype(jnp.bfloat16)
    preact = jnp.dot(hidden, weight, preferred_element_type=jnp.float32) + bias_vector
    sigmoid_pre = jax.nn.sigmoid(preact)
    activated = (preact * sigmoid_pre).astype(jnp.bfloat16)
    dpre = (upstream.astype(jnp.float32) * sigmoid_pre * (1.0 + preact * (1.0 - sigmoid_pre))).astype(jnp.bfloat16)
    scale_factor = 1.0 / jnp.sqrt(jnp.float32(node_total))
    grad_weight = jnp.dot(hidden.T, dpre, preferred_element_type=jnp.float32) * scale_factor
    grad_bias = lax.optimization_barrier(jnp.sum(dpre.astype(jnp.float32), axis=0)) * scale_factor
    dhidden = jnp.dot(dpre, weight.T, preferred_element_type=jnp.float32).astype(jnp.bfloat16)
    grad_blocks = dhidden.reshape(node_total // BLOCK, BLOCK, width)

    def backward_one(totals, device):
        picked = grad_blocks[row_global[device]].astype(jnp.float32)
        chosen = jnp.where(live_mask[device][:, None, None], block_tiles[device], jnp.zeros_like(block_tiles[device])).astype(jnp.float32)
        product = jnp.einsum('sji,sjh->sih', chosen, picked)
        return (totals.at[col_global[device]].add(product), None)
    grad_sum, unused = lax.scan(backward_one, zero_blocks, jnp.arange(devices_all, dtype=jnp.int32))
    grad_features = grad_sum.reshape(node_total, width).astype(jnp.bfloat16)
    return (activated, grad_weight, grad_bias, grad_features)
```

```python
import math

import jax
import jax.numpy as jnp
from jax import lax
from jax.experimental import pallas as pl
from jax.experimental.pallas import tpu as pltpu
from jax.sharding import PartitionSpec as P

F32 = jnp.float32
BF16 = jnp.bfloat16
VMEM_LIMIT = 56 * 1024 * 1024
EXTRA_ROWS = 16


def vmem():
    return pl.BlockSpec(memory_space=pltpu.VMEM)


def smem():
    return pl.BlockSpec(memory_space=pltpu.SMEM)


def anywhere():
    return pl.BlockSpec(memory_space=pl.ANY)


def cost(flops, nbytes):
    return pl.CostEstimate(flops=int(flops), bytes_accessed=int(nbytes), transcendentals=0)


def params():
    return pltpu.CompilerParams(vmem_limit_bytes=VMEM_LIMIT)


def tree_sum(parts):
    while len(parts) > 1:
        half = len(parts) // 2
        parts = [parts[i] + parts[i + half] for i in range(half)]
    return parts[0]


class Layout:
    def __init__(self, row_size, col_size):
        self.rows, self.cols = row_size, col_size
        self.slow = math.gcd(row_size, 4)
        self.fast = row_size // self.slow
        self.cores = 2
        self.pairs = col_size // self.cores

    def move(self, a, slow=0, fast=0, pair=0, core=0):
        row = lambda r: ((r // self.fast + slow) % self.slow) * self.fast + (r % self.fast + fast) % self.fast
        col = lambda c: ((c // 2 + pair) % self.pairs) * 2 + (c % 2 + core) % 2
        if pair == 0 and core == 0:
            return lax.ppermute(a, "row", [(r, row(r)) for r in range(self.rows)])
        if slow == 0 and fast == 0:
            return lax.ppermute(a, "col", [(c, col(c)) for c in range(self.cols)])
        n = self.cols
        return lax.ppermute(
            a, ("row", "col"), [(r * n + c, row(r) * n + col(c)) for r in range(self.rows) for c in range(n)]
        )

    def position(self):
        r, c = lax.axis_index("row"), lax.axis_index("col")
        return r // self.fast, r % self.fast, c // 2, c % 2


def forward_product(lay, index_own, index_other, tiles_own, tiles_other, pieces, out_rows):
    slots, block, _ = tiles_own.shape
    _, node_dev, half = pieces[0].shape
    group = math.gcd(slots, 4)

    def kernel(io_ref, ix_ref, ao_ref, ax_ref, *refs):
        piece_refs, (out_ref, feats, total, sems) = refs[: lay.rows], refs[lay.rows :]
        z, y, _, _ = lay.position()
        copies = []
        for dz in range(lay.slow):
            for dy in range(lay.fast):
                at = lax.rem(z - dz + lay.slow, lay.slow) * lay.fast + lax.rem(y - dy + lay.fast, lay.fast)
                n = dz * lay.fast + dy
                copies.append(
                    pltpu.make_async_copy(
                        piece_refs[n],
                        feats.at[:, pl.ds(pl.multiple_of(at * node_dev, node_dev), node_dev), :],
                        sems.at[n],
                    )
                )
        for c in copies:
            c.start()
        total[...] = jnp.zeros_like(total)
        for c in copies:
            c.wait()
        for which, (idx, tiles) in enumerate(((io_ref, ao_ref), (ix_ref, ax_ref))):
            count = idx[2 * slots]

            def turn(g, carry, which=which, idx=idx, tiles=tiles, count=count):
                products = []
                for j in range(group):
                    s = g * group + j
                    at = pl.multiple_of(idx[slots + s] * block, block)
                    p = jnp.dot(tiles[s], feats[which, pl.ds(at, block), :], preferred_element_type=F32)
                    products.append(jnp.where(s < count, p, 0.0))
                for j, p in enumerate(products):
                    to = pl.multiple_of(idx[g * group + j] * block, block)
                    total[pl.ds(to, block), :] += p
                return carry

            lax.fori_loop(0, (count + group - 1) // group, turn, 0)
        out_ref[...] = total[...].astype(BF16)

    return pl.pallas_call(
        kernel,
        out_shape=jax.ShapeDtypeStruct((out_rows, half), BF16),
        in_specs=[smem(), smem(), vmem(), vmem()] + [anywhere()] * lay.rows,
        out_specs=vmem(),
        scratch_shapes=[
            pltpu.VMEM((2, lay.rows * node_dev, half), BF16),
            pltpu.VMEM((out_rows, half), F32),
            pltpu.SemaphoreType.DMA((lay.rows,)),
        ],
        compiler_params=params(),
        cost_estimate=cost(4 * slots * block * block * half, 4 * lay.rows * node_dev * half),
        name="forward_product",
    )(index_own, index_other, tiles_own, tiles_other, *pieces)


def dense_part(lay, hidden_own, hidden_other, weight, bias, ups):
    rows, half = hidden_own.shape
    width = weight.shape[0]
    node_dev = ups[0].shape[0]
    share = half // lay.pairs
    part = share // lay.fast

    def kernel(ho_ref, hx_ref, w_ref, b_ref, *refs):
        up_refs, refs = refs[: lay.cols], refs[lay.cols :]
        act_ref, dh_ref, refs = refs[0], refs[1], refs[2:]
        gw_refs, (up_all, gw, sems) = refs[: lay.fast], refs[lay.fast :]
        _, y, x, k = lay.position()
        copies = []
        for dx in range(lay.pairs):
            for dk in range(2):
                at = lax.rem(x - dx + lay.pairs, lay.pairs) * 2 + lax.rem(k + dk, 2)
                n = dx * 2 + dk
                copies.append(
                    pltpu.make_async_copy(
                        up_refs[n],
                        up_all.at[pl.ds(pl.multiple_of(at * node_dev, node_dev), node_dev), :],
                        sems.at[n],
                    )
                )
        for c in copies:
            c.start()
        for c in copies:
            c.wait()
        gb = jnp.zeros((1, width), F32)
        for j in range(lay.cols):
            sl = pl.ds(j * node_dev, node_dev)
            ho, hx = ho_ref[sl, :], hx_ref[sl, :]
            h = jnp.concatenate([jnp.where(k == 0, ho, hx), jnp.where(k == 0, hx, ho)], axis=1)
            pre = jnp.dot(h, w_ref[...], preferred_element_type=F32) + b_ref[...]
            sig = jax.nn.sigmoid(pre)

            @pl.when(x * 2 + k == j)
            def _(pre=pre, sig=sig):
                act_ref[...] = (pre * sig).astype(BF16)

            dpre = (up_all[sl, :].astype(F32) * sig * (1.0 + pre * (1.0 - sig))).astype(BF16)
            gb += jnp.sum(dpre.astype(F32), axis=0, keepdims=True)
            one = lax.dot_general(ho, dpre, (((0,), (0,)), ((), ())), preferred_element_type=F32)
            if j == 0:
                gw[...] = one
            else:
                gw[...] += one
            dh_ref[sl, :] = lax.dot_general(
                dpre, w_ref[...], (((1,), (1,)), ((), ())), preferred_element_type=F32
            ).astype(BF16)
        high = gb.astype(BF16).astype(F32)
        low = gb - high
        line = lax.broadcasted_iota(jnp.int32, (EXTRA_ROWS, width), 0)
        extra = jnp.where(line == 0, high, jnp.where(line == 1, low, 0.0)).astype(BF16)
        for dy in range(lay.fast):
            at = x * share + lax.rem(y + dy, lay.fast) * part
            gw_refs[dy][:part, :] = gw[pl.ds(pl.multiple_of(at, part), part), :].astype(BF16)
            gw_refs[dy][part:, :] = extra

    return pl.pallas_call(
        kernel,
        out_shape=[
            jax.ShapeDtypeStruct((node_dev, width), BF16),
            jax.ShapeDtypeStruct((rows, width), BF16),
        ]
        + [jax.ShapeDtypeStruct((part + EXTRA_ROWS, width), BF16)] * lay.fast,
        in_specs=[vmem()] * 4 + [anywhere()] * lay.cols,
        out_specs=[vmem()] * (2 + lay.fast),
        scratch_shapes=[
            pltpu.VMEM((rows, width), BF16),
            pltpu.VMEM((half, width), F32),
            pltpu.SemaphoreType.DMA((lay.cols,)),
        ],
        compiler_params=params(),
        cost_estimate=cost(5 * rows * width * width, 6 * rows * width),
        name="dense_part",
    )(hidden_own, hidden_other, weight, bias, *ups)


def backward_product(lay, index_own, tiles_own, dhidden, node_dev):
    slots, block, _ = tiles_own.shape
    rows, width = dhidden.shape
    group = math.gcd(slots, 4)

    def kernel(idx, tiles, dh_ref, *refs):
        out_refs, (total,) = refs[: lay.rows], refs[lay.rows :]
        z, y, _, _ = lay.position()
        total[...] = jnp.zeros_like(total)
        count = idx[2 * slots]

        def turn(g, carry):
            products = []
            for j in range(group):
                s = g * group + j
                at = pl.multiple_of(idx[s] * block, block)
                p = lax.dot_general(
                    tiles[s], dh_ref[pl.ds(at, block), :], (((0,), (0,)), ((), ())), preferred_element_type=F32
                )
                products.append(jnp.where(s < count, p, 0.0))
            for j, p in enumerate(products):
                to = pl.multiple_of(idx[slots + g * group + j] * block, block)
                total[pl.ds(to, block), :] += p
            return carry

        lax.fori_loop(0, (count + group - 1) // group, turn, 0)
        for dz in range(lay.slow):
            for dy in range(lay.fast):
                at = lax.rem(z + dz, lay.slow) * lay.fast + lax.rem(y + dy, lay.fast)
                out_refs[dz * lay.fast + dy][...] = total[
                    pl.ds(pl.multiple_of(at * node_dev, node_dev), node_dev), :
                ].astype(BF16)

    return pl.pallas_call(
        kernel,
        out_shape=[jax.ShapeDtypeStruct((node_dev, width), BF16)] * lay.rows,
        in_specs=[smem(), vmem(), vmem()],
        out_specs=[vmem()] * lay.rows,
        scratch_shapes=[pltpu.VMEM((lay.rows * node_dev, width), F32)],
        compiler_params=params(),
        cost_estimate=cost(2 * slots * block * block * width, 2 * lay.rows * node_dev * width),
        name="backward_product",
    )(index_own, tiles_own, dhidden)


def place_weight_gradient(lay, own, other, width):
    half = width // 2
    share = half // lay.pairs
    part = share // lay.fast

    def kernel(own_ref, other_ref, out_ref):
        _, y, x, k = lay.position()
        for dk, ref in enumerate((own_ref, other_ref)):
            for dx in range(lay.pairs):
                for dy in range(lay.fast):
                    n = dx * lay.fast + dy
                    at = (
                        lax.rem(k + dk, 2) * half
                        + lax.rem(x - dx + lay.pairs, lay.pairs) * share
                        + lax.rem(y - dy + lay.fast, lay.fast) * part
                    )
                    out_ref[pl.ds(pl.multiple_of(at, part), part), :] = ref[n * part : (n + 1) * part, :].astype(F32)

    return pl.pallas_call(
        kernel,
        out_shape=jax.ShapeDtypeStruct((width, width), F32),
        in_specs=[vmem(), vmem()],
        out_specs=vmem(),
        compiler_params=params(),
        cost_estimate=cost(width * width, 6 * width * width),
        name="place_weight_gradient",
    )(own, other)


def shards(features, blocks, block_rows, block_cols, block_count, weight, bias_vector, upstream):
    lay = Layout(lax.axis_size("row"), lax.axis_size("col"))
    node_dev, width = features.shape
    half = width // 2
    scale = 1.0 / math.sqrt(node_dev * lay.rows * lay.cols)
    tiles = blocks[0, 0]
    core = lax.axis_index("col") % 2

    index = jnp.concatenate([block_rows[0, 0], block_cols[0, 0], block_count[0]])
    low, high = features[:, :half], features[:, half:]
    keep = jnp.where(core == 0, low, high)
    give = jnp.where(core == 0, high, low)
    piece = jnp.stack([keep, lay.move(give, core=1)])
    index_other = lay.move(index, core=1)
    tiles_other = lay.move(tiles, core=1)

    gathered = {(0, 0): piece}
    for dz in [0] + [d for d in (1, 3, 2) if d < lay.slow]:
        if dz:
            gathered[dz, 0] = lay.move(piece, slow=dz)
        for dy in range(1, lay.fast):
            gathered[dz, dy] = lay.move(gathered[dz, 0], fast=dy)
    pieces = [gathered[dz, dy] for dz in range(lay.slow) for dy in range(lay.fast)]

    ups = [upstream, lay.move(upstream, core=1)]
    for dx in range(1, lay.pairs):
        ups.append(lay.move(upstream, pair=dx))
        ups.append(lay.move(ups[-1], core=1))

    partial_sum = forward_product(lay, index, index_other, tiles, tiles_other, pieces, node_dev * lay.cols)
    arrived = [partial_sum] + [lay.move(partial_sum, pair=dx) for dx in range(1, lay.pairs)]
    hidden_own = tree_sum([a.astype(F32) for a in arrived]).astype(BF16)
    hidden_other = lay.move(hidden_own, core=1)

    activated, dhidden, *gw_parts = dense_part(lay, hidden_own, hidden_other, weight, bias_vector[None], ups)

    gw = [gw_parts[0]] + [lay.move(gw_parts[dy], fast=dy) for dy in range(1, lay.fast)]
    gw_sum = tree_sum([g.astype(F32) for g in gw])
    gb_sum = gw_sum[-EXTRA_ROWS:]
    gb_line = gb_sum[0] + gb_sum[1]
    gb_high = gb_line.astype(BF16)
    gb_low = (gb_line - gb_high.astype(F32)).astype(BF16)
    line = jnp.arange(EXTRA_ROWS)[:, None]
    gb_rows = jnp.where(line == 0, gb_high[None], jnp.where(line == 1, gb_low[None], jnp.zeros((), BF16)))
    gw_send = jnp.concatenate([gw_sum[:-EXTRA_ROWS].astype(BF16), gb_rows])
    gw_all = tree_sum([g.astype(F32) for g in [gw_send] + [lay.move(gw_send, slow=dz) for dz in range(1, lay.slow)]])
    gw_all = gw_all * scale
    grad_bias = gw_all[-EXTRA_ROWS] + gw_all[1 - EXTRA_ROWS]
    gw_final = gw_all[:-EXTRA_ROWS].astype(BF16)
    shares = []
    for dx in range(lay.pairs):
        for dy in range(lay.fast):
            shares.append(gw_final if dx == 0 and dy == 0 else lay.move(gw_final, pair=dx, fast=dy))
    gw_own = jnp.concatenate(shares)
    grad_weight = place_weight_gradient(lay, gw_own, lay.move(gw_own, core=1), width)

    outs = backward_product(lay, index, tiles, dhidden, node_dev)
    sums = {}
    for dz in [d for d in (2, 1, 3, 0) if d < lay.slow]:
        s = outs[dz * lay.fast].astype(F32)
        for dy in range(1, lay.fast):
            s = s + lay.move(outs[dz * lay.fast + dy], fast=dy).astype(F32)
        sums[dz] = lay.move(s.astype(BF16), slow=dz).astype(F32) if dz else s
    grad = sums[0]
    for dz in range(1, lay.slow):
        grad = grad + sums[dz]
    return (activated, grad_weight, grad_bias, grad.astype(BF16))


def solution(mesh):
    in_specs = (
        P(("col", "row"), None),
        P("row", "col", None, None, None),
        P("row", "col", None),
        P("row", "col", None),
        P("row", "col"),
        P(),
        P(),
        P(("row", "col"), None),
    )
    out_specs = (P(("row", "col"), None), P(), P(), P(("col", "row"), None))
    return jax.shard_map(shards, mesh=mesh, in_specs=in_specs, out_specs=out_specs, check_vma=False)
```

```python
import math

import jax
import jax.numpy as jnp
from jax import lax
from jax.experimental import pallas as pl
from jax.experimental.pallas import tpu as pltpu
from jax.sharding import PartitionSpec as P

F32 = jnp.float32
BF16 = jnp.bfloat16
VMEM_LIMIT = 40 * 1024 * 1024
EXTRA_ROWS = 16


def vmem():
    return pl.BlockSpec(memory_space=pltpu.VMEM)


def smem():
    return pl.BlockSpec(memory_space=pltpu.SMEM)


def hbm():
    return pl.BlockSpec(memory_space=pl.ANY)


def cost(flops, nbytes):
    return pl.CostEstimate(flops=int(flops), bytes_accessed=int(nbytes), transcendentals=0)


def params():
    return pltpu.CompilerParams(vmem_limit_bytes=VMEM_LIMIT)


def xor_to(index, distance):
    return lax.bitwise_xor(index, jnp.int32(distance))


def tree_sum(parts):
    while len(parts) > 1:
        half = len(parts) // 2
        parts = [parts[i] + parts[i + half] for i in range(half)]
    return parts[0]


class Layout:
    def __init__(self, row_size, col_size):
        self.rows, self.cols = row_size, col_size
        self.slow = math.gcd(row_size, 4)
        self.fast = row_size // self.slow
        self.pairs = col_size // 2
        assert row_size & (row_size - 1) == 0 and col_size & (col_size - 1) == 0 and col_size > 1

    def move_row(self, a, slow=0, fast=0):
        d = slow * self.fast + fast
        return lax.ppermute(a, "row", [(r, r ^ d) for r in range(self.rows)])

    def move_col(self, a, pair=0, core=0):
        d = pair * 2 + core
        return lax.ppermute(a, "col", [(c, c ^ d) for c in range(self.cols)])


def forward_product(lay, index_own, index_other, tiles_own, tiles_other, pieces, out_rows):
    slots, block, _ = tiles_own.shape
    _, node_dev, half = pieces[0].shape
    group = math.gcd(slots, 4)

    def kernel(io_ref, ix_ref, ao_ref, ax_ref, *refs):
        piece_refs, (out_a, out_b, feats, total, sems) = refs[: lay.rows], refs[lay.rows :]
        row = lax.axis_index("row")
        copies = []
        for d in range(lay.rows):
            at = pl.multiple_of(xor_to(row, d) * node_dev, node_dev)
            copies.append(pltpu.make_async_copy(piece_refs[d], feats.at[:, pl.ds(at, node_dev), :], sems.at[d]))
        for c in copies:
            c.start()
        total[...] = jnp.zeros_like(total)
        for c in copies:
            c.wait()
        for which, (idx, tiles) in enumerate(((io_ref, ao_ref), (ix_ref, ax_ref))):
            count = idx[2 * slots]

            def turn(g, carry, which=which, idx=idx, tiles=tiles, count=count):
                products = []
                for j in range(group):
                    s = g * group + j
                    at = pl.multiple_of(idx[slots + s] * block, block)
                    p = jnp.dot(tiles[s], feats[which, pl.ds(at, block), :], preferred_element_type=F32)
                    products.append(jnp.where(s < count, p, 0.0))
                for j, p in enumerate(products):
                    to = pl.multiple_of(idx[g * group + j] * block, block)
                    total[pl.ds(to, block), :] += p
                return carry

            lax.fori_loop(0, (count + group - 1) // group, turn, 0)
        out_a[...] = total[: out_rows // 2, :].astype(BF16)
        out_b[...] = total[out_rows // 2 :, :].astype(BF16)

    return pl.pallas_call(
        kernel,
        out_shape=[jax.ShapeDtypeStruct((out_rows // 2, half), BF16)] * 2,
        in_specs=[smem(), smem(), vmem(), vmem()] + [hbm()] * lay.rows,
        out_specs=[vmem()] * 2,
        scratch_shapes=[
            pltpu.VMEM((2, lay.rows * node_dev, half), BF16),
            pltpu.VMEM((out_rows, half), F32),
            pltpu.SemaphoreType.DMA((lay.rows,)),
        ],
        compiler_params=params(),
        cost_estimate=cost(4 * slots * block * block * half, 4 * lay.rows * node_dev * half),
        name="forward_product",
    )(index_own, index_other, tiles_own, tiles_other, *pieces)


def dense_and_backward(lay, sums, weight, bias, index_own, tiles_own, ups):
    node_dev, width = ups[0].shape
    rows, half = node_dev * lay.cols, width // 2
    share = half // lay.pairs
    slots, block, _ = tiles_own.shape
    group = math.gcd(slots, 4)

    n_sums = len(sums)

    def kernel(w_ref, b_ref, idx, tiles, *refs):
        up_refs, sum_refs, refs = refs[: lay.cols], refs[lay.cols :][:n_sums], refs[lay.cols + n_sums :]
        act_ref, gw_ref, refs = refs[0], refs[1], refs[2:]
        out_refs, (up_all, parts, hidden, gw, dh_ref, total, sems) = refs[: lay.rows], refs[lay.rows :]
        row, col = lax.axis_index("row"), lax.axis_index("col")
        pair, core = col // 2, lax.rem(col, 2)
        copies = []
        for d in range(lay.cols):
            at = pl.multiple_of(xor_to(col, d) * node_dev, node_dev)
            copies.append(pltpu.make_async_copy(up_refs[d], up_all.at[pl.ds(at, node_dev), :], sems.at[d]))
        for n, ref in enumerate(sum_refs):
            part, dk, dx = n % 2, n // 2 % 2, n // 4
            at = pl.multiple_of(xor_to(core, dk) * half, half)
            to = parts.at[dx, pl.ds(part * (rows // 2), rows // 2), pl.ds(at, half)]
            copies.append(pltpu.make_async_copy(ref, to, sems.at[lay.cols + n]))
        for c in copies:
            c.start()
        total[...] = jnp.zeros_like(total)
        for c in copies:
            c.wait()
        own_half = pl.ds(pl.multiple_of(core * half, half), half)
        gb = jnp.zeros((1, width), F32)
        for j in range(lay.cols):
            sl = pl.ds(j * node_dev, node_dev)
            h = tree_sum([parts[dx, sl, :].astype(F32) for dx in range(lay.pairs)]).astype(BF16)
            hidden[sl, :] = h
            pre = jnp.dot(h, w_ref[...], preferred_element_type=F32) + b_ref[...]
            sig = jax.nn.sigmoid(pre)

            @pl.when(col == j)
            def _(pre=pre, sig=sig):
                act_ref[...] = (pre * sig).astype(BF16)

            dpre = (up_all[sl, :].astype(F32) * sig * (1.0 + pre * (1.0 - sig))).astype(BF16)
            gb += jnp.sum(dpre.astype(F32), axis=0, keepdims=True)
            one = lax.dot_general(hidden[sl, own_half], dpre, (((0,), (0,)), ((), ())), preferred_element_type=F32)
            if j == 0:
                gw[...] = one
            else:
                gw[...] += one
            dh_ref[sl, :] = lax.dot_general(
                dpre, w_ref[...], (((1,), (1,)), ((), ())), preferred_element_type=F32
            ).astype(BF16)
        high = gb.astype(BF16).astype(F32)
        low = gb - high
        line = lax.broadcasted_iota(jnp.int32, (EXTRA_ROWS, width), 0)
        extra = jnp.where(line == 0, high, jnp.where(line == 1, low, 0.0)).astype(BF16)
        gw_ref[:share, :] = gw[pl.ds(pl.multiple_of(pair * share, share), share), :].astype(BF16)
        gw_ref[share:, :] = extra

        count = idx[2 * slots]

        def turn(g, carry):
            products = []
            for j in range(group):
                s = g * group + j
                at = pl.multiple_of(idx[s] * block, block)
                p = lax.dot_general(
                    tiles[s], dh_ref[pl.ds(at, block), :], (((0,), (0,)), ((), ())), preferred_element_type=F32
                )
                products.append(jnp.where(s < count, p, 0.0))
            for j, p in enumerate(products):
                to = pl.multiple_of(idx[slots + g * group + j] * block, block)
                total[pl.ds(to, block), :] += p
            return carry

        lax.fori_loop(0, (count + group - 1) // group, turn, 0)
        for d in range(lay.rows):
            at = pl.multiple_of(xor_to(row, d) * node_dev, node_dev)
            out_refs[d][...] = total[pl.ds(at, node_dev), :].astype(BF16)

    return pl.pallas_call(
        kernel,
        out_shape=[
            jax.ShapeDtypeStruct((node_dev, width), BF16),
            jax.ShapeDtypeStruct((share + EXTRA_ROWS, width), BF16),
        ]
        + [jax.ShapeDtypeStruct((node_dev, width), BF16)] * lay.rows,
        in_specs=[vmem(), vmem(), smem(), vmem()] + [hbm()] * (lay.cols + n_sums),
        out_specs=[vmem()] * (2 + lay.rows),
        scratch_shapes=[
            pltpu.VMEM((rows, width), BF16),
            pltpu.VMEM((lay.pairs, rows, width), BF16),
            pltpu.VMEM((rows, width), BF16),
            pltpu.VMEM((half, width), F32),
            pltpu.VMEM((rows, width), BF16),
            pltpu.VMEM((lay.rows * node_dev, width), F32),
            pltpu.SemaphoreType.DMA((lay.cols + n_sums,)),
        ],
        compiler_params=params(),
        cost_estimate=cost(5 * rows * width * width, 8 * rows * width),
        name="dense_and_backward",
    )(weight, bias, index_own, tiles_own, *ups, *sums)


def place_weight_gradient(lay, own, other, width):
    half = width // 2
    share = half // lay.pairs

    def kernel(*refs):
        own_refs, other_refs, out_ref = refs[: lay.pairs], refs[lay.pairs : 2 * lay.pairs], refs[-1]
        col = lax.axis_index("col")
        pair, core = col // 2, lax.rem(col, 2)
        for dk, shares in enumerate((own_refs, other_refs)):
            for dx in range(lay.pairs):
                at = pl.multiple_of(xor_to(core, dk) * half + xor_to(pair, dx) * share, share)
                out_ref[pl.ds(at, share), :] = shares[dx][...].astype(F32)

    return pl.pallas_call(
        kernel,
        out_shape=jax.ShapeDtypeStruct((width, width), F32),
        in_specs=[vmem()] * (2 * lay.pairs),
        out_specs=vmem(),
        compiler_params=params(),
        cost_estimate=cost(width * width, 6 * width * width),
        name="place_weight_gradient",
    )(*own, *other)


def split_bias(total, width):
    line_sum = total[-EXTRA_ROWS] + total[1 - EXTRA_ROWS]
    high = line_sum.astype(BF16)
    low = (line_sum - high.astype(F32)).astype(BF16)
    line = jnp.arange(EXTRA_ROWS)[:, None]
    extra = jnp.where(line == 0, high[None], jnp.where(line == 1, low[None], jnp.zeros((), BF16)))
    return jnp.concatenate([total[:-EXTRA_ROWS].astype(BF16), extra])


def shards(features, blocks, block_rows, block_cols, block_count, weight, bias_vector, upstream):
    lay = Layout(lax.axis_size("row"), lax.axis_size("col"))
    node_dev, width = features.shape
    half = width // 2
    scale = 1.0 / math.sqrt(node_dev * lay.rows * lay.cols)
    tiles = blocks[0, 0]
    core = lax.axis_index("col") % 2

    index = jnp.concatenate([block_rows[0, 0], block_cols[0, 0], block_count[0]])
    low, high = features[:, :half], features[:, half:]
    keep = jnp.where(core == 0, low, high)
    give = jnp.where(core == 0, high, low)
    piece = jnp.stack([keep, lay.move_col(give, core=1)])

    piece, upstream = lax.optimization_barrier((piece, upstream))
    gathered = {0: piece}

    def over_fast(dz):
        for dy in range(1, lay.fast):
            gathered[dz * lay.fast + dy] = lay.move_row(gathered[dz * lay.fast], fast=dy)

    def over_fast_of(dz):
        return [gathered[dz * lay.fast + dy] for dy in range(1, lay.fast)]

    for dz in reversed(range(1, lay.slow)):
        if dz & (dz - 1) == 0:
            gathered[dz * lay.fast] = lay.move_row(piece, slow=dz)
    over_fast(0)
    far_ups = [lay.move_col(upstream, pair=dx, core=dk) for dx in range(1, lay.pairs) for dk in range(2)]
    one = lay.fast if lay.slow > 1 else 0
    near, gathered[one], own_upstream, own_index, own_tiles = lax.optimization_barrier(
        (over_fast_of(0), gathered[one], upstream, index, tiles)
    )
    gathered.update(zip(range(1, lay.fast), near))
    index_other = lay.move_col(own_index, core=1)
    tiles_other = lay.move_col(own_tiles, core=1)
    near_up = lay.move_col(own_upstream, core=1)
    for dz in range(1, lay.slow):
        top = 1 << (dz.bit_length() - 1)
        if dz != top:
            source, far_ups = lax.optimization_barrier((gathered[top * lay.fast], far_ups))
            gathered[top * lay.fast] = source
            gathered[dz * lay.fast] = lay.move_row(source, slow=dz ^ top)
    others = (index_other, tiles_other, near_up)
    for dz in range(1, lay.slow):
        over_fast(dz)
        if dz < lay.slow - 1:
            after = (dz + 1) * lay.fast
            extra = others if dz == lay.slow - 2 else ()
            gathered[after], done, extra = lax.optimization_barrier((gathered[after], over_fast_of(dz), extra))
            gathered.update(zip(range(dz * lay.fast + 1, after), done))
            others = extra or others
    index_other, tiles_other, near_up = others
    ups = [upstream, near_up] + list(far_ups)
    pieces = [gathered[d] for d in range(lay.rows)]

    mine = forward_product(lay, index, index_other, tiles, tiles_other, pieces, node_dev * lay.cols)
    sums = list(mine) + [lay.move_col(a, core=1) for a in mine]
    for dx in range(1, lay.pairs):
        came = [lay.move_col(a, pair=dx) for a in mine]
        sums += came + [lay.move_col(a, core=1) for a in came]

    activated, gw, *outs = dense_and_backward(
        lay, sums, weight, bias_vector[None], index, tiles, ups
    )

    def fast_sum(dz):
        arrived = [lay.move_row(outs[dz * lay.fast + dy], fast=dy) for dy in range(1, lay.fast)]
        return sum([a.astype(F32) for a in arrived], outs[dz * lay.fast].astype(F32))

    def hold(dz, until):
        span = slice(dz * lay.fast + 1, (dz + 1) * lay.fast)
        until, outs[span] = lax.optimization_barrier((until, outs[span]))
        return until

    hops = [dict(slow=1 << i) for i in range(lay.slow.bit_length() - 1)]
    hops += [dict(fast=1 << i) for i in range(lay.fast.bit_length() - 1)]
    sums = {dz: fast_sum(dz) for dz in range(2, lay.slow)}
    came = None
    for n, hop in enumerate(hops):
        if n:
            gw = split_bias(gw.astype(F32) + came.astype(F32), width)
            if hop.get("fast") == 1 and lay.slow > 2:
                gw, sums[2] = lax.optimization_barrier((gw, sums[2]))
            if hop.get("fast") == 1 and lay.slow > 1:
                gw = hold(1, gw)
        came = lay.move_row(gw, **hop)
    came = hold(0, came)
    for dz in range(min(2, lay.slow)):
        sums[dz] = fast_sum(dz)
    for dz in reversed(range(1, lay.slow)):
        top = 1 << (dz.bit_length() - 1)
        to, hop = (top, dz ^ top) if dz != top else (0, dz)
        sums[to] = sums[to] + lay.move_row(sums[dz].astype(BF16), slow=hop).astype(F32)
    grad_features = sums[0].astype(BF16)

    total = (gw.astype(F32) + came.astype(F32)) * scale
    grad_bias = total[-EXTRA_ROWS] + total[1 - EXTRA_ROWS]
    share = total[:-EXTRA_ROWS].astype(BF16)
    own = [share] + [lay.move_col(share, pair=dx) for dx in range(1, lay.pairs)]
    other = lay.move_col(jnp.stack(own), core=1)
    grad_weight = place_weight_gradient(lay, own, [other[i] for i in range(lay.pairs)], width)
    return (activated, grad_weight, grad_bias, grad_features)


def solution(mesh):
    in_specs = (
        P(("col", "row"), None),
        P("row", "col", None, None, None),
        P("row", "col", None),
        P("row", "col", None),
        P("row", "col"),
        P(),
        P(),
        P(("row", "col"), None),
    )
    out_specs = (P(("row", "col"), None), P(), P(), P(("col", "row"), None))
    return jax.shard_map(shards, mesh=mesh, in_specs=in_specs, out_specs=out_specs, check_vma=False)
```

```python
import math

import jax
import jax.numpy as jnp
from jax import lax
from jax.experimental import pallas as pl
from jax.experimental.pallas import tpu as pltpu
from jax.sharding import PartitionSpec as P

F32 = jnp.float32
BF16 = jnp.bfloat16
VMEM_LIMIT = 40 * 1024 * 1024
EXTRA_ROWS = 16


def vmem():
    return pl.BlockSpec(memory_space=pltpu.VMEM)


def smem():
    return pl.BlockSpec(memory_space=pltpu.SMEM)


def hbm():
    return pl.BlockSpec(memory_space=pl.ANY)


def cost(flops, nbytes):
    return pl.CostEstimate(flops=int(flops), bytes_accessed=int(nbytes), transcendentals=0)


def params():
    return pltpu.CompilerParams(vmem_limit_bytes=VMEM_LIMIT)


def xor_to(index, distance):
    return lax.bitwise_xor(index, jnp.int32(distance))


def tree_sum(parts):
    while len(parts) > 1:
        half = len(parts) // 2
        parts = [parts[i] + parts[i + half] for i in range(half)]
    return parts[0]


class Layout:
    def __init__(self, row_size, col_size):
        self.rows, self.cols = row_size, col_size
        self.slow = math.gcd(row_size, 4)
        self.fast = row_size // self.slow
        self.pairs = col_size // 2
        assert row_size & (row_size - 1) == 0 and col_size & (col_size - 1) == 0 and col_size > 1

    def move_row(self, a, slow=0, fast=0):
        d = slow * self.fast + fast
        return lax.ppermute(a, "row", [(r, r ^ d) for r in range(self.rows)])

    def move_col(self, a, pair=0, core=0):
        d = pair * 2 + core
        return lax.ppermute(a, "col", [(c, c ^ d) for c in range(self.cols)])


def forward_product(lay, index_own, index_other, tiles_own, tiles_other, pieces, out_rows):
    slots, block, _ = tiles_own.shape
    _, node_dev, half = pieces[0].shape
    group = math.gcd(slots, 4)

    def kernel(io_ref, ix_ref, ao_ref, ax_ref, *refs):
        piece_refs, (out_a, out_b, feats, total, sems) = refs[: lay.rows], refs[lay.rows :]
        row = lax.axis_index("row")
        copies = []
        for d in range(lay.rows):
            at = pl.multiple_of(xor_to(row, d) * node_dev, node_dev)
            copies.append(pltpu.make_async_copy(piece_refs[d], feats.at[:, pl.ds(at, node_dev), :], sems.at[d]))
        for c in copies:
            c.start()
        total[...] = jnp.zeros_like(total)
        for c in copies:
            c.wait()
        for which, (idx, tiles) in enumerate(((io_ref, ao_ref), (ix_ref, ax_ref))):
            count = idx[2 * slots]

            def turn(g, carry, which=which, idx=idx, tiles=tiles, count=count):
                products = []
                for j in range(group):
                    s = g * group + j
                    at = pl.multiple_of(idx[slots + s] * block, block)
                    p = jnp.dot(tiles[s], feats[which, pl.ds(at, block), :], preferred_element_type=F32)
                    products.append(jnp.where(s < count, p, 0.0))
                for j, p in enumerate(products):
                    to = pl.multiple_of(idx[g * group + j] * block, block)
                    total[pl.ds(to, block), :] += p
                return carry

            lax.fori_loop(0, (count + group - 1) // group, turn, 0)
        out_a[...] = total[: out_rows // 2, :].astype(BF16)
        out_b[...] = total[out_rows // 2 :, :].astype(BF16)

    return pl.pallas_call(
        kernel,
        out_shape=[jax.ShapeDtypeStruct((out_rows // 2, half), BF16)] * 2,
        in_specs=[smem(), smem(), vmem(), vmem()] + [hbm()] * lay.rows,
        out_specs=[vmem()] * 2,
        scratch_shapes=[
            pltpu.VMEM((2, lay.rows * node_dev, half), BF16),
            pltpu.VMEM((out_rows, half), F32),
            pltpu.SemaphoreType.DMA((lay.rows,)),
        ],
        compiler_params=params(),
        cost_estimate=cost(4 * slots * block * block * half, 4 * lay.rows * node_dev * half),
        name="forward_product",
    )(index_own, index_other, tiles_own, tiles_other, *pieces)


def dense_and_backward(lay, sums, weight, bias, index_own, tiles_own, ups):
    node_dev, width = ups[0].shape
    rows, half = node_dev * lay.cols, width // 2
    share = half // lay.pairs
    slots, block, _ = tiles_own.shape
    group = math.gcd(slots, 4)

    n_sums = len(sums)

    def kernel(w_ref, b_ref, idx, tiles, *refs):
        up_refs, sum_refs, refs = refs[: lay.cols], refs[lay.cols :][:n_sums], refs[lay.cols + n_sums :]
        act_ref, gw_ref, refs = refs[0], refs[1], refs[2:]
        out_refs, (up_all, parts, hidden, gw, dh_ref, total, sems) = refs[: lay.rows], refs[lay.rows :]
        row, col = lax.axis_index("row"), lax.axis_index("col")
        pair, core = col // 2, lax.rem(col, 2)
        copies = []
        for d in range(lay.cols):
            at = pl.multiple_of(xor_to(col, d) * node_dev, node_dev)
            copies.append(pltpu.make_async_copy(up_refs[d], up_all.at[pl.ds(at, node_dev), :], sems.at[d]))
        for n, ref in enumerate(sum_refs):
            part, dk, dx = n % 2, n // 2 % 2, n // 4
            at = pl.multiple_of(xor_to(core, dk) * half, half)
            to = parts.at[dx, pl.ds(part * (rows // 2), rows // 2), pl.ds(at, half)]
            copies.append(pltpu.make_async_copy(ref, to, sems.at[lay.cols + n]))
        for c in copies:
            c.start()
        total[...] = jnp.zeros_like(total)
        for c in copies:
            c.wait()
        own_half = pl.ds(pl.multiple_of(core * half, half), half)
        gb = jnp.zeros((1, width), F32)
        for j in range(lay.cols):
            sl = pl.ds(j * node_dev, node_dev)
            h = tree_sum([parts[dx, sl, :].astype(F32) for dx in range(lay.pairs)]).astype(BF16)
            hidden[sl, :] = h
            pre = jnp.dot(h, w_ref[...], preferred_element_type=F32) + b_ref[...]
            sig = jax.nn.sigmoid(pre)

            @pl.when(col == j)
            def _(pre=pre, sig=sig):
                act_ref[...] = (pre * sig).astype(BF16)

            dpre = (up_all[sl, :].astype(F32) * sig * (1.0 + pre * (1.0 - sig))).astype(BF16)
            gb += jnp.sum(dpre.astype(F32), axis=0, keepdims=True)
            one = lax.dot_general(hidden[sl, own_half], dpre, (((0,), (0,)), ((), ())), preferred_element_type=F32)
            if j == 0:
                gw[...] = one
            else:
                gw[...] += one
            dh_ref[sl, :] = lax.dot_general(
                dpre, w_ref[...], (((1,), (1,)), ((), ())), preferred_element_type=F32
            ).astype(BF16)
        high = gb.astype(BF16).astype(F32)
        low = gb - high
        line = lax.broadcasted_iota(jnp.int32, (EXTRA_ROWS, width), 0)
        extra = jnp.where(line == 0, high, jnp.where(line == 1, low, 0.0)).astype(BF16)
        gw_ref[:share, :] = gw[pl.ds(pl.multiple_of(pair * share, share), share), :].astype(BF16)
        gw_ref[share:, :] = extra

        count = idx[2 * slots]

        def turn(g, carry):
            products = []
            for j in range(group):
                s = g * group + j
                at = pl.multiple_of(idx[s] * block, block)
                p = lax.dot_general(
                    tiles[s], dh_ref[pl.ds(at, block), :], (((0,), (0,)), ((), ())), preferred_element_type=F32
                )
                products.append(jnp.where(s < count, p, 0.0))
            for j, p in enumerate(products):
                to = pl.multiple_of(idx[slots + g * group + j] * block, block)
                total[pl.ds(to, block), :] += p
            return carry

        lax.fori_loop(0, (count + group - 1) // group, turn, 0)
        for d in range(lay.rows):
            at = pl.multiple_of(xor_to(row, d) * node_dev, node_dev)
            out_refs[d][...] = total[pl.ds(at, node_dev), :].astype(BF16)

    return pl.pallas_call(
        kernel,
        out_shape=[
            jax.ShapeDtypeStruct((node_dev, width), BF16),
            jax.ShapeDtypeStruct((share + EXTRA_ROWS, width), BF16),
        ]
        + [jax.ShapeDtypeStruct((node_dev, width), BF16)] * lay.rows,
        in_specs=[vmem(), vmem(), smem(), vmem()] + [hbm()] * (lay.cols + n_sums),
        out_specs=[vmem()] * (2 + lay.rows),
        scratch_shapes=[
            pltpu.VMEM((rows, width), BF16),
            pltpu.VMEM((lay.pairs, rows, width), BF16),
            pltpu.VMEM((rows, width), BF16),
            pltpu.VMEM((half, width), F32),
            pltpu.VMEM((rows, width), BF16),
            pltpu.VMEM((lay.rows * node_dev, width), F32),
            pltpu.SemaphoreType.DMA((lay.cols + n_sums,)),
        ],
        compiler_params=params(),
        cost_estimate=cost(5 * rows * width * width, 8 * rows * width),
        name="dense_and_backward",
    )(weight, bias, index_own, tiles_own, *ups, *sums)


def place_weight_gradient(lay, own, other, width):
    half = width // 2
    share = half // lay.pairs

    def kernel(*refs):
        own_refs, other_refs, out_ref = refs[: lay.pairs], refs[lay.pairs : 2 * lay.pairs], refs[-1]
        col = lax.axis_index("col")
        pair, core = col // 2, lax.rem(col, 2)
        for dk, shares in enumerate((own_refs, other_refs)):
            for dx in range(lay.pairs):
                at = pl.multiple_of(xor_to(core, dk) * half + xor_to(pair, dx) * share, share)
                out_ref[pl.ds(at, share), :] = shares[dx][...].astype(F32)

    return pl.pallas_call(
        kernel,
        out_shape=jax.ShapeDtypeStruct((width, width), F32),
        in_specs=[vmem()] * (2 * lay.pairs),
        out_specs=vmem(),
        compiler_params=params(),
        cost_estimate=cost(width * width, 6 * width * width),
        name="place_weight_gradient",
    )(*own, *other)


def split_bias(total, width):
    line_sum = total[-EXTRA_ROWS] + total[1 - EXTRA_ROWS]
    high = line_sum.astype(BF16)
    low = (line_sum - high.astype(F32)).astype(BF16)
    line = jnp.arange(EXTRA_ROWS)[:, None]
    extra = jnp.where(line == 0, high[None], jnp.where(line == 1, low[None], jnp.zeros((), BF16)))
    return jnp.concatenate([total[:-EXTRA_ROWS].astype(BF16), extra])


def shards(features, blocks, block_rows, block_cols, block_count, weight, bias_vector, upstream):
    lay = Layout(lax.axis_size("row"), lax.axis_size("col"))
    node_dev, width = features.shape
    half = width // 2
    scale = 1.0 / math.sqrt(node_dev * lay.rows * lay.cols)
    tiles = blocks[0, 0]
    core = lax.axis_index("col") % 2

    index = jnp.concatenate([block_rows[0, 0], block_cols[0, 0], block_count[0]])
    low, high = features[:, :half], features[:, half:]
    keep = jnp.where(core == 0, low, high)
    give = jnp.where(core == 0, high, low)
    piece = jnp.stack([keep, lay.move_col(give, core=1)])

    piece, upstream = lax.optimization_barrier((piece, upstream))
    gathered = {0: piece}

    def over_fast(dz):
        for dy in range(1, lay.fast):
            gathered[dz * lay.fast + dy] = lay.move_row(gathered[dz * lay.fast], fast=dy)

    def over_fast_of(dz):
        return [gathered[dz * lay.fast + dy] for dy in range(1, lay.fast)]

    for dz in reversed(range(1, lay.slow)):
        if dz & (dz - 1) == 0:
            gathered[dz * lay.fast] = lay.move_row(piece, slow=dz)
    over_fast(0)
    far_ups = [lay.move_col(upstream, pair=dx, core=dk) for dx in range(1, lay.pairs) for dk in range(2)]
    one = lay.fast if lay.slow > 1 else 0
    near, gathered[one], own_upstream, own_index, own_tiles = lax.optimization_barrier(
        (over_fast_of(0), gathered[one], upstream, index, tiles)
    )
    gathered.update(zip(range(1, lay.fast), near))
    index_other = lay.move_col(own_index, core=1)
    tiles_other = lay.move_col(own_tiles, core=1)
    near_up = lay.move_col(own_upstream, core=1)
    for dz in range(1, lay.slow):
        top = 1 << (dz.bit_length() - 1)
        if dz != top:
            gathered[dz * lay.fast] = lay.move_row(gathered[top * lay.fast], slow=dz ^ top)
    others = (index_other, tiles_other, near_up, far_ups)
    for dz in range(1, lay.slow):
        over_fast(dz)
        if dz < lay.slow - 1:
            after = (dz + 1) * lay.fast
            extra = others if dz == lay.slow - 2 else ()
            gathered[after], done, extra = lax.optimization_barrier((gathered[after], over_fast_of(dz), extra))
            gathered.update(zip(range(dz * lay.fast + 1, after), done))
            others = extra or others
    index_other, tiles_other, near_up, far_ups = others
    ups = [upstream, near_up] + list(far_ups)
    pieces = [gathered[d] for d in range(lay.rows)]

    mine = forward_product(lay, index, index_other, tiles, tiles_other, pieces, node_dev * lay.cols)
    sums = list(mine) + [lay.move_col(a, core=1) for a in mine]
    for dx in range(1, lay.pairs):
        came = [lay.move_col(a, pair=dx) for a in mine]
        sums += came + [lay.move_col(a, core=1) for a in came]

    activated, gw, *outs = dense_and_backward(
        lay, sums, weight, bias_vector[None], index, tiles, ups
    )

    def fast_arrivals(dz):
        return [lay.move_row(outs[dz * lay.fast + dy], fast=dy) for dy in range(1, lay.fast)]

    def fast_sum(dz, arrived):
        return sum([a.astype(F32) for a in arrived], outs[dz * lay.fast].astype(F32))

    def hold(dz, until):
        span = slice(dz * lay.fast + 1, (dz + 1) * lay.fast)
        until, outs[span] = lax.optimization_barrier((until, outs[span]))
        return until

    def slow_sum(dz):
        top = 1 << (dz.bit_length() - 1)
        to, hop = (top, dz ^ top) if dz != top else (0, dz)
        sums[to] = sums[to] + lay.move_row(sums[dz].astype(BF16), slow=hop).astype(F32)

    hops = [dict(slow=1 << i) for i in range(lay.slow.bit_length() - 1)]
    hops += [dict(fast=1 << i) for i in range(lay.fast.bit_length() - 1)]
    sums = {}
    if lay.slow > 2:
        sums[3] = hold(2, fast_sum(3, fast_arrivals(3)).astype(BF16))
        sums[2] = fast_sum(2, fast_arrivals(2))
        slow_sum(3)
    came = None
    for n, hop in enumerate(hops):
        if n:
            gw = split_bias(gw.astype(F32) + came.astype(F32), width)
            if hop.get("fast") == 1 and lay.slow > 2:
                gw = hold(1, gw)
                gw, sums[2] = lax.optimization_barrier((gw, sums[2]))
        came = lay.move_row(gw, **hop)
    came = hold(0, came)
    for dz in range(min(2, lay.slow)):
        sums[dz] = fast_sum(dz, fast_arrivals(dz))
    for dz in reversed(range(1, min(3, lay.slow))):
        slow_sum(dz)
    grad_features = sums[0].astype(BF16)

    total = (gw.astype(F32) + came.astype(F32)) * scale
    grad_bias = total[-EXTRA_ROWS] + total[1 - EXTRA_ROWS]
    share = total[:-EXTRA_ROWS].astype(BF16)
    own = [share] + [lay.move_col(share, pair=dx) for dx in range(1, lay.pairs)]
    other = lay.move_col(jnp.stack(own), core=1)
    grad_weight = place_weight_gradient(lay, own, [other[i] for i in range(lay.pairs)], width)
    return (activated, grad_weight, grad_bias, grad_features)


def solution(mesh):
    in_specs = (
        P(("col", "row"), None),
        P("row", "col", None, None, None),
        P("row", "col", None),
        P("row", "col", None),
        P("row", "col"),
        P(),
        P(),
        P(("row", "col"), None),
    )
    out_specs = (P(("row", "col"), None), P(), P(), P(("col", "row"), None))
    return jax.shard_map(shards, mesh=mesh, in_specs=in_specs, out_specs=out_specs, check_vma=False)
```

```python
import math

import jax
import jax.numpy as jnp
from jax import lax
from jax.experimental import pallas as pl
from jax.experimental.pallas import tpu as pltpu
from jax.sharding import PartitionSpec as P

F32 = jnp.float32
BF16 = jnp.bfloat16
VMEM_LIMIT = 40 * 1024 * 1024
EXTRA_ROWS = 16


def vmem():
    return pl.BlockSpec(memory_space=pltpu.VMEM)


def smem():
    return pl.BlockSpec(memory_space=pltpu.SMEM)


def hbm():
    return pl.BlockSpec(memory_space=pl.ANY)


def cost(flops, nbytes):
    return pl.CostEstimate(flops=int(flops), bytes_accessed=int(nbytes), transcendentals=0)


def params():
    return pltpu.CompilerParams(vmem_limit_bytes=VMEM_LIMIT)


def xor_to(index, distance):
    return lax.bitwise_xor(index, jnp.int32(distance))


def tree_sum(parts):
    while len(parts) > 1:
        half = len(parts) // 2
        parts = [parts[i] + parts[i + half] for i in range(half)]
    return parts[0]


class Layout:
    def __init__(self, row_size, col_size):
        self.rows, self.cols = row_size, col_size
        self.slow = math.gcd(row_size, 4)
        self.fast = row_size // self.slow
        self.pairs = col_size // 2
        assert row_size & (row_size - 1) == 0 and col_size & (col_size - 1) == 0 and col_size > 1

    def move_row(self, a, slow=0, fast=0):
        d = slow * self.fast + fast
        return lax.ppermute(a, "row", [(r, r ^ d) for r in range(self.rows)])

    def move_col(self, a, pair=0, core=0):
        d = pair * 2 + core
        return lax.ppermute(a, "col", [(c, c ^ d) for c in range(self.cols)])


def forward_product(lay, index_own, index_other, tiles_own, tiles_other, pieces, out_rows):
    slots, block, _ = tiles_own.shape
    _, node_dev, half = pieces[0].shape
    group = math.gcd(slots, 4)

    def kernel(io_ref, ix_ref, ao_ref, ax_ref, *refs):
        piece_refs, (out_a, out_b, feats, total, sems) = refs[: lay.rows], refs[lay.rows :]
        row = lax.axis_index("row")
        copies = []
        for d in range(lay.rows):
            at = pl.multiple_of(xor_to(row, d) * node_dev, node_dev)
            copies.append(pltpu.make_async_copy(piece_refs[d], feats.at[:, pl.ds(at, node_dev), :], sems.at[d]))
        for c in copies:
            c.start()
        total[...] = jnp.zeros_like(total)
        for c in copies:
            c.wait()
        for which, (idx, tiles) in enumerate(((io_ref, ao_ref), (ix_ref, ax_ref))):
            count = idx[2 * slots]

            def turn(g, carry, which=which, idx=idx, tiles=tiles, count=count):
                products = []
                for j in range(group):
                    s = g * group + j
                    at = pl.multiple_of(idx[slots + s] * block, block)
                    p = jnp.dot(tiles[s], feats[which, pl.ds(at, block), :], preferred_element_type=F32)
                    products.append(jnp.where(s < count, p, 0.0))
                for j, p in enumerate(products):
                    to = pl.multiple_of(idx[g * group + j] * block, block)
                    total[pl.ds(to, block), :] += p
                return carry

            lax.fori_loop(0, (count + group - 1) // group, turn, 0)
        out_a[...] = total[: out_rows // 2, :].astype(BF16)
        out_b[...] = total[out_rows // 2 :, :].astype(BF16)

    return pl.pallas_call(
        kernel,
        out_shape=[jax.ShapeDtypeStruct((out_rows // 2, half), BF16)] * 2,
        in_specs=[smem(), smem(), vmem(), vmem()] + [hbm()] * lay.rows,
        out_specs=[vmem()] * 2,
        scratch_shapes=[
            pltpu.VMEM((2, lay.rows * node_dev, half), BF16),
            pltpu.VMEM((out_rows, half), F32),
            pltpu.SemaphoreType.DMA((lay.rows,)),
        ],
        compiler_params=params(),
        cost_estimate=cost(4 * slots * block * block * half, 4 * lay.rows * node_dev * half),
        name="forward_product",
    )(index_own, index_other, tiles_own, tiles_other, *pieces)


def dense_and_backward(lay, sums, weight, bias, index_own, tiles_own, ups, ups_other):
    node_dev, width = ups[0].shape
    rows, half = node_dev * lay.cols, width // 2
    share = half // lay.pairs
    slots, block, _ = tiles_own.shape
    group = math.gcd(slots, 4)

    n_sums = len(sums)

    def kernel(w_ref, b_ref, idx, tiles, *refs):
        n_ups = lay.pairs + 1
        up_refs, sum_refs, refs = refs[:n_ups], refs[n_ups:][:n_sums], refs[n_ups + n_sums :]
        act_ref, gw_ref, refs = refs[0], refs[1], refs[2:]
        out_refs, (up_all, parts, hidden, gw, dh_ref, total, sems) = refs[: lay.rows], refs[lay.rows :]
        row, col = lax.axis_index("row"), lax.axis_index("col")
        pair, core = col // 2, lax.rem(col, 2)
        copies = []
        for d in range(lay.cols):
            at = pl.multiple_of(xor_to(col, d) * node_dev, node_dev)
            ref = up_refs[-1].at[d // 2] if d % 2 else up_refs[d // 2]
            copies.append(pltpu.make_async_copy(ref, up_all.at[pl.ds(at, node_dev), :], sems.at[d]))
        for n, ref in enumerate(sum_refs):
            part, dk, dx = n % 2, n // 2 % 2, n // 4
            at = pl.multiple_of(xor_to(core, dk) * half, half)
            to = parts.at[dx, pl.ds(part * (rows // 2), rows // 2), pl.ds(at, half)]
            copies.append(pltpu.make_async_copy(ref, to, sems.at[lay.cols + n]))
        for c in copies:
            c.start()
        total[...] = jnp.zeros_like(total)
        for c in copies:
            c.wait()
        own_half = pl.ds(pl.multiple_of(core * half, half), half)
        gb = jnp.zeros((1, width), F32)
        for j in range(lay.cols):
            sl = pl.ds(j * node_dev, node_dev)
            h = tree_sum([parts[dx, sl, :].astype(F32) for dx in range(lay.pairs)]).astype(BF16)
            hidden[sl, :] = h
            pre = jnp.dot(h, w_ref[...], preferred_element_type=F32) + b_ref[...]
            sig = jax.nn.sigmoid(pre)

            @pl.when(col == j)
            def _(pre=pre, sig=sig):
                act_ref[...] = (pre * sig).astype(BF16)

            dpre = (up_all[sl, :].astype(F32) * sig * (1.0 + pre * (1.0 - sig))).astype(BF16)
            gb += jnp.sum(dpre.astype(F32), axis=0, keepdims=True)
            one = lax.dot_general(hidden[sl, own_half], dpre, (((0,), (0,)), ((), ())), preferred_element_type=F32)
            if j == 0:
                gw[...] = one
            else:
                gw[...] += one
            dh_ref[sl, :] = lax.dot_general(
                dpre, w_ref[...], (((1,), (1,)), ((), ())), preferred_element_type=F32
            ).astype(BF16)
        high = gb.astype(BF16).astype(F32)
        low = gb - high
        line = lax.broadcasted_iota(jnp.int32, (EXTRA_ROWS, width), 0)
        extra = jnp.where(line == 0, high, jnp.where(line == 1, low, 0.0)).astype(BF16)
        gw_ref[:share, :] = gw[pl.ds(pl.multiple_of(pair * share, share), share), :].astype(BF16)
        gw_ref[share:, :] = extra

        count = idx[2 * slots]

        def turn(g, carry):
            products = []
            for j in range(group):
                s = g * group + j
                at = pl.multiple_of(idx[s] * block, block)
                p = lax.dot_general(
                    tiles[s], dh_ref[pl.ds(at, block), :], (((0,), (0,)), ((), ())), preferred_element_type=F32
                )
                products.append(jnp.where(s < count, p, 0.0))
            for j, p in enumerate(products):
                to = pl.multiple_of(idx[slots + g * group + j] * block, block)
                total[pl.ds(to, block), :] += p
            return carry

        lax.fori_loop(0, (count + group - 1) // group, turn, 0)
        for d in range(lay.rows):
            at = pl.multiple_of(xor_to(row, d) * node_dev, node_dev)
            out_refs[d][...] = total[pl.ds(at, node_dev), :].astype(BF16)

    return pl.pallas_call(
        kernel,
        out_shape=[
            jax.ShapeDtypeStruct((node_dev, width), BF16),
            jax.ShapeDtypeStruct((share + EXTRA_ROWS, width), BF16),
        ]
        + [jax.ShapeDtypeStruct((node_dev, width), BF16)] * lay.rows,
        in_specs=[vmem(), vmem(), smem(), vmem()] + [hbm()] * (lay.pairs + 1 + n_sums),
        out_specs=[vmem()] * (2 + lay.rows),
        scratch_shapes=[
            pltpu.VMEM((rows, width), BF16),
            pltpu.VMEM((lay.pairs, rows, width), BF16),
            pltpu.VMEM((rows, width), BF16),
            pltpu.VMEM((half, width), F32),
            pltpu.VMEM((rows, width), BF16),
            pltpu.VMEM((lay.rows * node_dev, width), F32),
            pltpu.SemaphoreType.DMA((lay.cols + n_sums,)),
        ],
        compiler_params=params(),
        cost_estimate=cost(5 * rows * width * width, 8 * rows * width),
        name="dense_and_backward",
    )(weight, bias, index_own, tiles_own, *ups, ups_other, *sums)


def place_weight_gradient(lay, own, other, width):
    half = width // 2
    share = half // lay.pairs

    def kernel(*refs):
        own_refs, other_refs, out_ref = refs[: lay.pairs], refs[lay.pairs : 2 * lay.pairs], refs[-1]
        col = lax.axis_index("col")
        pair, core = col // 2, lax.rem(col, 2)
        for dk, shares in enumerate((own_refs, other_refs)):
            for dx in range(lay.pairs):
                at = pl.multiple_of(xor_to(core, dk) * half + xor_to(pair, dx) * share, share)
                out_ref[pl.ds(at, share), :] = shares[dx][...].astype(F32)

    return pl.pallas_call(
        kernel,
        out_shape=jax.ShapeDtypeStruct((width, width), F32),
        in_specs=[vmem()] * (2 * lay.pairs),
        out_specs=vmem(),
        compiler_params=params(),
        cost_estimate=cost(width * width, 6 * width * width),
        name="place_weight_gradient",
    )(*own, *other)


def split_bias(total, width):
    line_sum = total[-EXTRA_ROWS] + total[1 - EXTRA_ROWS]
    high = line_sum.astype(BF16)
    low = (line_sum - high.astype(F32)).astype(BF16)
    line = jnp.arange(EXTRA_ROWS)[:, None]
    extra = jnp.where(line == 0, high[None], jnp.where(line == 1, low[None], jnp.zeros((), BF16)))
    return jnp.concatenate([total[:-EXTRA_ROWS].astype(BF16), extra])


def shards(features, blocks, block_rows, block_cols, block_count, weight, bias_vector, upstream):
    lay = Layout(lax.axis_size("row"), lax.axis_size("col"))
    node_dev, width = features.shape
    half = width // 2
    scale = 1.0 / math.sqrt(node_dev * lay.rows * lay.cols)
    tiles = blocks[0, 0]
    core = lax.axis_index("col") % 2

    mine = [jnp.where(core == 0, a[:, :half], a[:, half:]) for a in (features, lay.move_col(features, core=1))]
    piece = jnp.stack(mine)

    piece, upstream = lax.optimization_barrier((piece, upstream))
    gathered = {0: piece}

    def over_fast(dz):
        for dy in range(1, lay.fast):
            gathered[dz * lay.fast + dy] = lay.move_row(gathered[dz * lay.fast], fast=dy)

    def over_fast_of(dz):
        return [gathered[dz * lay.fast + dy] for dy in range(1, lay.fast)]

    for dz in reversed(range(1, lay.slow)):
        if dz & (dz - 1) == 0:
            gathered[dz * lay.fast] = lay.move_row(piece, slow=dz)
    over_fast(0)
    ups = [upstream] + [lay.move_col(upstream, pair=dx) for dx in range(1, lay.pairs)]
    one = lay.fast if lay.slow > 1 else 0
    near, gathered[one], later = lax.optimization_barrier(
        (over_fast_of(0), gathered[one], (block_rows, block_cols, block_count, tiles))
    )
    block_rows, block_cols, block_count, tiles = later
    index = jnp.concatenate([block_rows[0, 0], block_cols[0, 0], block_count[0]])
    gathered.update(zip(range(1, lay.fast), near))
    index_other = lay.move_col(index, core=1)
    tiles_other = lay.move_col(tiles, core=1)
    ups_other = lay.move_col(jnp.stack(ups), core=1)
    for dz in range(1, lay.slow):
        top = 1 << (dz.bit_length() - 1)
        if dz != top:
            gathered[dz * lay.fast] = lay.move_row(gathered[top * lay.fast], slow=dz ^ top)
    others = (index_other, tiles_other, ups_other)
    for dz in range(1, lay.slow):
        over_fast(dz)
        if dz < lay.slow - 1:
            after = (dz + 1) * lay.fast
            extra = others if dz == lay.slow - 2 else ()
            gathered[after], done, extra = lax.optimization_barrier((gathered[after], over_fast_of(dz), extra))
            gathered.update(zip(range(dz * lay.fast + 1, after), done))
            others = extra or others
    index_other, tiles_other, ups_other = others
    pieces = [gathered[d] for d in range(lay.rows)]

    mine = forward_product(lay, index, index_other, tiles, tiles_other, pieces, node_dev * lay.cols)
    sums = list(mine) + [lay.move_col(a, core=1) for a in mine]
    for dx in range(1, lay.pairs):
        came = [lay.move_col(a, pair=dx) for a in mine]
        sums += came + [lay.move_col(a, core=1) for a in came]

    activated, gw, *outs = dense_and_backward(
        lay, sums, weight, bias_vector[None], index, tiles, ups, ups_other
    )

    def fast_arrivals(dz):
        return [lay.move_row(outs[dz * lay.fast + dy], fast=dy) for dy in range(1, lay.fast)]

    def fast_sum(dz, arrived):
        return sum([a.astype(F32) for a in arrived], outs[dz * lay.fast].astype(F32))

    def hold(dz, until):
        span = slice(dz * lay.fast + 1, (dz + 1) * lay.fast)
        until, outs[span] = lax.optimization_barrier((until, outs[span]))
        return until

    def slow_sum(dz):
        top = 1 << (dz.bit_length() - 1)
        to, hop = (top, dz ^ top) if dz != top else (0, dz)
        sums[to] = sums[to] + lay.move_row(sums[dz].astype(BF16), slow=hop).astype(F32)

    hops = [dict(slow=1 << i) for i in range(lay.slow.bit_length() - 1)]
    hops += [dict(fast=1 << i) for i in range(lay.fast.bit_length() - 1)]
    sums = {}
    if lay.slow > 2:
        sums[3] = hold(2, fast_sum(3, fast_arrivals(3)).astype(BF16))
        sums[2] = fast_sum(2, fast_arrivals(2))
        slow_sum(3)
    came = None
    for n, hop in enumerate(hops):
        if n:
            gw = split_bias(gw.astype(F32) + came.astype(F32), width)
            if hop.get("fast") == 1 and lay.slow > 2:
                gw = hold(1, gw)
                gw, sums[2] = lax.optimization_barrier((gw, sums[2]))
        came = lay.move_row(gw, **hop)
    came = hold(0, came)
    for dz in range(min(2, lay.slow)):
        sums[dz] = fast_sum(dz, fast_arrivals(dz))
    for dz in reversed(range(1, min(3, lay.slow))):
        slow_sum(dz)
    grad_features = sums[0].astype(BF16)

    total = (gw.astype(F32) + came.astype(F32)) * scale
    grad_bias = total[-EXTRA_ROWS] + total[1 - EXTRA_ROWS]
    share = total[:-EXTRA_ROWS].astype(BF16)
    own = [share] + [lay.move_col(share, pair=dx) for dx in range(1, lay.pairs)]
    other = lay.move_col(jnp.stack(own), core=1)
    grad_weight = place_weight_gradient(lay, own, [other[i] for i in range(lay.pairs)], width)
    return (activated, grad_weight, grad_bias, grad_features)


def solution(mesh):
    in_specs = (
        P(("col", "row"), None),
        P("row", "col", None, None, None),
        P("row", "col", None),
        P("row", "col", None),
        P("row", "col"),
        P(),
        P(),
        P(("row", "col"), None),
    )
    out_specs = (P(("row", "col"), None), P(), P(), P(("col", "row"), None))
    return jax.shard_map(shards, mesh=mesh, in_specs=in_specs, out_specs=out_specs, check_vma=False)
```

```python
import math

import jax
import jax.numpy as jnp
from jax import lax
from jax.experimental import pallas as pl
from jax.experimental.pallas import tpu as pltpu
from jax.sharding import PartitionSpec as P

F32 = jnp.float32
BF16 = jnp.bfloat16
VMEM_LIMIT = 40 * 1024 * 1024
EXTRA_ROWS = 16


def vmem():
    return pl.BlockSpec(memory_space=pltpu.VMEM)


def smem():
    return pl.BlockSpec(memory_space=pltpu.SMEM)


def hbm():
    return pl.BlockSpec(memory_space=pl.ANY)


def cost(flops, nbytes):
    return pl.CostEstimate(flops=int(flops), bytes_accessed=int(nbytes), transcendentals=0)


def params():
    return pltpu.CompilerParams(vmem_limit_bytes=VMEM_LIMIT)


def xor_to(index, distance):
    return lax.bitwise_xor(index, jnp.int32(distance))


def tree_sum(parts):
    while len(parts) > 1:
        half = len(parts) // 2
        parts = [parts[i] + parts[i + half] for i in range(half)]
    return parts[0]


class Layout:
    def __init__(self, row_size, col_size):
        self.rows, self.cols = row_size, col_size
        self.slow = math.gcd(row_size, 4)
        self.fast = row_size // self.slow
        self.pairs = col_size // 2
        assert row_size & (row_size - 1) == 0 and col_size & (col_size - 1) == 0 and col_size > 1

    def move_row(self, a, slow=0, fast=0):
        d = slow * self.fast + fast
        return lax.ppermute(a, "row", [(r, r ^ d) for r in range(self.rows)])

    def move_col(self, a, pair=0, core=0):
        d = pair * 2 + core
        return lax.ppermute(a, "col", [(c, c ^ d) for c in range(self.cols)])


def forward_product(lay, index_own, index_other, tiles_own, tiles_other, pieces, out_rows):
    slots, block, _ = tiles_own.shape
    _, node_dev, half = pieces[0].shape
    group = math.gcd(slots, 4)

    def kernel(io_ref, ix_ref, ao_ref, ax_ref, *refs):
        piece_refs, (out_a, out_b, feats, total, sems) = refs[: lay.rows], refs[lay.rows :]
        row = lax.axis_index("row")
        copies = []
        for d in range(lay.rows):
            at = pl.multiple_of(xor_to(row, d) * node_dev, node_dev)
            copies.append(pltpu.make_async_copy(piece_refs[d], feats.at[:, pl.ds(at, node_dev), :], sems.at[d]))
        for c in copies:
            c.start()
        total[...] = jnp.zeros_like(total)
        for c in copies:
            c.wait()
        for which, (idx, tiles) in enumerate(((io_ref, ao_ref), (ix_ref, ax_ref))):
            count = idx[2 * slots]

            def turn(g, carry, which=which, idx=idx, tiles=tiles, count=count):
                products = []
                for j in range(group):
                    s = g * group + j
                    at = pl.multiple_of(idx[slots + s] * block, block)
                    p = jnp.dot(tiles[s], feats[which, pl.ds(at, block), :], preferred_element_type=F32)
                    products.append(jnp.where(s < count, p, 0.0))
                for j, p in enumerate(products):
                    to = pl.multiple_of(idx[g * group + j] * block, block)
                    total[pl.ds(to, block), :] += p
                return carry

            lax.fori_loop(0, (count + group - 1) // group, turn, 0)
        out_a[...] = total[: out_rows // 2, :].astype(BF16)
        out_b[...] = total[out_rows // 2 :, :].astype(BF16)

    return pl.pallas_call(
        kernel,
        out_shape=[jax.ShapeDtypeStruct((out_rows // 2, half), BF16)] * 2,
        in_specs=[smem(), smem(), vmem(), vmem()] + [hbm()] * lay.rows,
        out_specs=[vmem()] * 2,
        scratch_shapes=[
            pltpu.VMEM((2, lay.rows * node_dev, half), BF16),
            pltpu.VMEM((out_rows, half), F32),
            pltpu.SemaphoreType.DMA((lay.rows,)),
        ],
        compiler_params=params(),
        cost_estimate=cost(4 * slots * block * block * half, 4 * lay.rows * node_dev * half),
        name="forward_product",
    )(index_own, index_other, tiles_own, tiles_other, *pieces)


def dense_and_backward(lay, sums, weight, bias, index_own, tiles_own, ups, ups_other):
    node_dev, width = ups[0].shape
    rows, half = node_dev * lay.cols, width // 2
    share = half // lay.pairs
    slots, block, _ = tiles_own.shape
    group = math.gcd(slots, 4)

    n_sums = len(sums)

    def kernel(w_ref, b_ref, idx, tiles, *refs):
        n_ups = lay.pairs + 1
        up_refs, sum_refs, refs = refs[:n_ups], refs[n_ups:][:n_sums], refs[n_ups + n_sums :]
        act_ref, gw_ref, refs = refs[0], refs[1], refs[2:]
        out_refs, (up_all, parts, hidden, gw, dh_ref, total, sems) = refs[: lay.rows], refs[lay.rows :]
        row, col = lax.axis_index("row"), lax.axis_index("col")
        pair, core = col // 2, lax.rem(col, 2)
        copies = []
        for d in range(lay.cols):
            at = pl.multiple_of(xor_to(col, d) * node_dev, node_dev)
            ref = up_refs[-1].at[d // 2] if d % 2 else up_refs[d // 2]
            copies.append(pltpu.make_async_copy(ref, up_all.at[pl.ds(at, node_dev), :], sems.at[d]))
        for n, ref in enumerate(sum_refs):
            part, dk, dx = n % 2, n // 2 % 2, n // 4
            at = pl.multiple_of(xor_to(core, dk) * half, half)
            to = parts.at[dx, pl.ds(part * (rows // 2), rows // 2), pl.ds(at, half)]
            copies.append(pltpu.make_async_copy(ref, to, sems.at[lay.cols + n]))
        for c in copies:
            c.start()
        total[...] = jnp.zeros_like(total)
        for c in copies:
            c.wait()
        own_half = pl.ds(pl.multiple_of(core * half, half), half)
        gb = jnp.zeros((1, width), F32)
        for j in range(lay.cols):
            sl = pl.ds(j * node_dev, node_dev)
            h = tree_sum([parts[dx, sl, :].astype(F32) for dx in range(lay.pairs)]).astype(BF16)
            hidden[sl, :] = h
            pre = jnp.dot(h, w_ref[...], preferred_element_type=F32) + b_ref[...]
            sig = jax.nn.sigmoid(pre)

            @pl.when(col == j)
            def _(pre=pre, sig=sig):
                act_ref[...] = (pre * sig).astype(BF16)

            dpre = (up_all[sl, :].astype(F32) * sig * (1.0 + pre * (1.0 - sig))).astype(BF16)
            gb += jnp.sum(dpre.astype(F32), axis=0, keepdims=True)
            one = lax.dot_general(hidden[sl, own_half], dpre, (((0,), (0,)), ((), ())), preferred_element_type=F32)
            if j == 0:
                gw[...] = one
            else:
                gw[...] += one
            dh_ref[sl, :] = lax.dot_general(
                dpre, w_ref[...], (((1,), (1,)), ((), ())), preferred_element_type=F32
            ).astype(BF16)
        high = gb.astype(BF16).astype(F32)
        low = gb - high
        line = lax.broadcasted_iota(jnp.int32, (EXTRA_ROWS, width), 0)
        extra = jnp.where(line == 0, high, jnp.where(line == 1, low, 0.0)).astype(BF16)
        gw_ref[:share, :] = gw[pl.ds(pl.multiple_of(pair * share, share), share), :].astype(BF16)
        gw_ref[share:, :] = extra

        count = idx[2 * slots]

        def turn(g, carry):
            products = []
            for j in range(group):
                s = g * group + j
                at = pl.multiple_of(idx[s] * block, block)
                p = lax.dot_general(
                    tiles[s], dh_ref[pl.ds(at, block), :], (((0,), (0,)), ((), ())), preferred_element_type=F32
                )
                products.append(jnp.where(s < count, p, 0.0))
            for j, p in enumerate(products):
                to = pl.multiple_of(idx[slots + g * group + j] * block, block)
                total[pl.ds(to, block), :] += p
            return carry

        lax.fori_loop(0, (count + group - 1) // group, turn, 0)
        for d in range(lay.rows):
            at = pl.multiple_of(xor_to(row, d) * node_dev, node_dev)
            out_refs[d][...] = total[pl.ds(at, node_dev), :].astype(BF16)

    return pl.pallas_call(
        kernel,
        out_shape=[
            jax.ShapeDtypeStruct((node_dev, width), BF16),
            jax.ShapeDtypeStruct((share + EXTRA_ROWS, width), BF16),
        ]
        + [jax.ShapeDtypeStruct((node_dev, width), BF16)] * lay.rows,
        in_specs=[vmem(), vmem(), smem(), vmem()] + [hbm()] * (lay.pairs + 1 + n_sums),
        out_specs=[vmem()] * (2 + lay.rows),
        scratch_shapes=[
            pltpu.VMEM((rows, width), BF16),
            pltpu.VMEM((lay.pairs, rows, width), BF16),
            pltpu.VMEM((rows, width), BF16),
            pltpu.VMEM((half, width), F32),
            pltpu.VMEM((rows, width), BF16),
            pltpu.VMEM((lay.rows * node_dev, width), F32),
            pltpu.SemaphoreType.DMA((lay.cols + n_sums,)),
        ],
        compiler_params=params(),
        cost_estimate=cost(5 * rows * width * width, 8 * rows * width),
        name="dense_and_backward",
    )(weight, bias, index_own, tiles_own, *ups, ups_other, *sums)


def place_weight_gradient(lay, own, other, width):
    half = width // 2
    share = half // lay.pairs

    def kernel(*refs):
        own_refs, other_refs, out_ref = refs[: lay.pairs], refs[lay.pairs : 2 * lay.pairs], refs[-1]
        col = lax.axis_index("col")
        pair, core = col // 2, lax.rem(col, 2)
        for dk, shares in enumerate((own_refs, other_refs)):
            for dx in range(lay.pairs):
                at = pl.multiple_of(xor_to(core, dk) * half + xor_to(pair, dx) * share, share)
                out_ref[pl.ds(at, share), :] = shares[dx][...].astype(F32)

    return pl.pallas_call(
        kernel,
        out_shape=jax.ShapeDtypeStruct((width, width), F32),
        in_specs=[vmem()] * (2 * lay.pairs),
        out_specs=vmem(),
        compiler_params=params(),
        cost_estimate=cost(width * width, 6 * width * width),
        name="place_weight_gradient",
    )(*own, *other)


def split_bias(total, width):
    line_sum = total[-EXTRA_ROWS] + total[1 - EXTRA_ROWS]
    high = line_sum.astype(BF16)
    low = (line_sum - high.astype(F32)).astype(BF16)
    line = jnp.arange(EXTRA_ROWS)[:, None]
    extra = jnp.where(line == 0, high[None], jnp.where(line == 1, low[None], jnp.zeros((), BF16)))
    return jnp.concatenate([total[:-EXTRA_ROWS].astype(BF16), extra])


def shards(features, blocks, block_rows, block_cols, block_count, weight, bias_vector, upstream):
    lay = Layout(lax.axis_size("row"), lax.axis_size("col"))
    node_dev, width = features.shape
    half = width // 2
    scale = 1.0 / math.sqrt(node_dev * lay.rows * lay.cols)
    tiles = blocks[0, 0]
    core = lax.axis_index("col") % 2

    mine = [jnp.where(core == 0, a[:, :half], a[:, half:]) for a in (features, lay.move_col(features, core=1))]
    piece = jnp.stack(mine)

    piece, upstream = lax.optimization_barrier((piece, upstream))
    gathered = {0: piece}

    def over_fast(dz):
        for dy in range(1, lay.fast):
            gathered[dz * lay.fast + dy] = lay.move_row(gathered[dz * lay.fast], fast=dy)

    def over_fast_of(dz):
        return [gathered[dz * lay.fast + dy] for dy in range(1, lay.fast)]

    for dz in reversed(range(1, lay.slow)):
        if dz & (dz - 1) == 0:
            gathered[dz * lay.fast] = lay.move_row(piece, slow=dz)
    over_fast(0)
    ups = [upstream] + [lay.move_col(upstream, pair=dx) for dx in range(1, lay.pairs)]
    one = lay.fast if lay.slow > 1 else 0
    near, gathered[one], later = lax.optimization_barrier(
        (over_fast_of(0), gathered[one], (block_rows, block_cols, block_count, tiles))
    )
    block_rows, block_cols, block_count, tiles = later
    index = jnp.concatenate([block_rows[0, 0], block_cols[0, 0], block_count[0]])
    gathered.update(zip(range(1, lay.fast), near))
    index_other = lay.move_col(index, core=1)
    tiles_other = lay.move_col(tiles, core=1)
    ups_other = lay.move_col(jnp.stack(ups), core=1)
    for dz in range(1, lay.slow):
        top = 1 << (dz.bit_length() - 1)
        if dz != top:
            gathered[dz * lay.fast] = lay.move_row(gathered[top * lay.fast], slow=dz ^ top)
    others = (index_other, tiles_other, ups_other)
    for dz in range(1, lay.slow):
        over_fast(dz)
        if dz < lay.slow - 1:
            after = (dz + 1) * lay.fast
            extra = others if dz == lay.slow - 2 else ()
            gathered[after], done, extra = lax.optimization_barrier((gathered[after], over_fast_of(dz), extra))
            gathered.update(zip(range(dz * lay.fast + 1, after), done))
            others = extra or others
    index_other, tiles_other, ups_other = others
    pieces = [gathered[d] for d in range(lay.rows)]

    mine = forward_product(lay, index, index_other, tiles, tiles_other, pieces, node_dev * lay.cols)
    sums = list(mine) + [lay.move_col(a, core=1) for a in mine]
    for dx in range(1, lay.pairs):
        came = [lay.move_col(a, pair=dx) for a in mine]
        sums += came + [lay.move_col(a, core=1) for a in came]

    activated, gw, *outs = dense_and_backward(
        lay, sums, weight, bias_vector[None], index, tiles, ups, ups_other
    )

    def fast_arrivals(dz):
        return [lay.move_row(outs[dz * lay.fast + dy], fast=dy) for dy in range(1, lay.fast)]

    def fast_sum(dz, arrived):
        return sum([a.astype(F32) for a in arrived], outs[dz * lay.fast].astype(F32))

    def hold(dz, until):
        span = slice(dz * lay.fast + 1, (dz + 1) * lay.fast)
        until, outs[span] = lax.optimization_barrier((until, outs[span]))
        return until

    def slow_sum(dz):
        top = 1 << (dz.bit_length() - 1)
        to, hop = (top, dz ^ top) if dz != top else (0, dz)
        sums[to] = sums[to] + lay.move_row(sums[dz].astype(BF16), slow=hop).astype(F32)

    hops = [dict(slow=1)] * (lay.slow > 1)
    hops += [dict(fast=1 << i) for i in range(lay.fast.bit_length() - 1)]
    hops += [dict(slow=2)] * (lay.slow > 2)
    sums = {}
    if lay.slow > 2:
        sums[3] = hold(2, fast_sum(3, fast_arrivals(3)).astype(BF16))
        sums[2] = fast_sum(2, fast_arrivals(2))
        slow_sum(3)
    came = None
    for n, hop in enumerate(hops):
        if n:
            gw = split_bias(gw.astype(F32) + came.astype(F32), width)
            if n == len(hops) - 1 and lay.slow > 2:
                gw = hold(1, gw)
        came = lay.move_row(gw, **hop)
    if lay.slow > 1:
        sums[1] = hold(0, fast_sum(1, fast_arrivals(1)).astype(BF16))
    for dz in sorted(sums, reverse=True):
        if dz < 3:
            came, sums[dz] = lax.optimization_barrier((came, sums[dz]))
    sums[0] = fast_sum(0, fast_arrivals(0))
    for dz in reversed(range(1, min(3, lay.slow))):
        slow_sum(dz)
    grad_features = sums[0].astype(BF16)

    total = (gw.astype(F32) + came.astype(F32)) * scale
    grad_bias = total[-EXTRA_ROWS] + total[1 - EXTRA_ROWS]
    share = total[:-EXTRA_ROWS].astype(BF16)
    own = [share] + [lay.move_col(share, pair=dx) for dx in range(1, lay.pairs)]
    other = lay.move_col(jnp.stack(own), core=1)
    grad_weight = place_weight_gradient(lay, own, [other[i] for i in range(lay.pairs)], width)
    return (activated, grad_weight, grad_bias, grad_features)


def solution(mesh):
    in_specs = (
        P(("col", "row"), None),
        P("row", "col", None, None, None),
        P("row", "col", None),
        P("row", "col", None),
        P("row", "col"),
        P(),
        P(),
        P(("row", "col"), None),
    )
    out_specs = (P(("row", "col"), None), P(), P(), P(("col", "row"), None))
    return jax.shard_map(shards, mesh=mesh, in_specs=in_specs, out_specs=out_specs, check_vma=False)
```

```python
import math

import jax
import jax.numpy as jnp
from jax import lax
from jax.experimental import pallas as pl
from jax.experimental.pallas import tpu as pltpu
from jax.sharding import PartitionSpec as P

F32 = jnp.float32
BF16 = jnp.bfloat16
VMEM_LIMIT = 40 * 1024 * 1024
EXTRA_ROWS = 16


def vmem():
    return pl.BlockSpec(memory_space=pltpu.VMEM)


def smem():
    return pl.BlockSpec(memory_space=pltpu.SMEM)


def hbm():
    return pl.BlockSpec(memory_space=pl.ANY)


def cost(flops, nbytes):
    return pl.CostEstimate(flops=int(flops), bytes_accessed=int(nbytes), transcendentals=0)


def params():
    return pltpu.CompilerParams(vmem_limit_bytes=VMEM_LIMIT)


def xor_to(index, distance):
    return lax.bitwise_xor(index, jnp.int32(distance))


def tree_sum(parts):
    while len(parts) > 1:
        half = len(parts) // 2
        parts = [parts[i] + parts[i + half] for i in range(half)]
    return parts[0]


class Layout:
    def __init__(self, row_size, col_size):
        self.rows, self.cols = row_size, col_size
        self.slow = math.gcd(row_size, 4)
        self.fast = row_size // self.slow
        self.pairs = col_size // 2
        assert row_size & (row_size - 1) == 0 and col_size & (col_size - 1) == 0 and col_size > 1

    def move_row(self, a, slow=0, fast=0):
        d = slow * self.fast + fast
        return lax.ppermute(a, "row", [(r, r ^ d) for r in range(self.rows)])

    def move_col(self, a, pair=0, core=0):
        d = pair * 2 + core
        return lax.ppermute(a, "col", [(c, c ^ d) for c in range(self.cols)])


def forward_product(lay, index_own, index_other, tiles_own, tiles_other, pieces, out_rows):
    slots, block, _ = tiles_own.shape
    _, node_dev, half = pieces[0].shape
    group = math.gcd(slots, 4)

    def kernel(io_ref, ix_ref, ao_ref, ax_ref, *refs):
        piece_refs, (out_a, out_b, feats, total, sems) = refs[: lay.rows], refs[lay.rows :]
        row = lax.axis_index("row")
        copies = []
        for d in range(lay.rows):
            at = pl.multiple_of(xor_to(row, d) * node_dev, node_dev)
            copies.append(pltpu.make_async_copy(piece_refs[d], feats.at[:, pl.ds(at, node_dev), :], sems.at[d]))
        for c in copies:
            c.start()
        total[...] = jnp.zeros_like(total)
        for c in copies:
            c.wait()
        for which, (idx, tiles) in enumerate(((io_ref, ao_ref), (ix_ref, ax_ref))):
            count = idx[2 * slots]

            def turn(g, carry, which=which, idx=idx, tiles=tiles, count=count):
                products = []
                for j in range(group):
                    s = g * group + j
                    at = pl.multiple_of(idx[slots + s] * block, block)
                    p = jnp.dot(tiles[s], feats[which, pl.ds(at, block), :], preferred_element_type=F32)
                    products.append(jnp.where(s < count, p, 0.0))
                for j, p in enumerate(products):
                    to = pl.multiple_of(idx[g * group + j] * block, block)
                    total[pl.ds(to, block), :] += p
                return carry

            lax.fori_loop(0, (count + group - 1) // group, turn, 0)
        out_a[...] = total[: out_rows // 2, :].astype(BF16)
        out_b[...] = total[out_rows // 2 :, :].astype(BF16)

    return pl.pallas_call(
        kernel,
        out_shape=[jax.ShapeDtypeStruct((out_rows // 2, half), BF16)] * 2,
        in_specs=[smem(), smem(), vmem(), vmem()] + [hbm()] * lay.rows,
        out_specs=[vmem()] * 2,
        scratch_shapes=[
            pltpu.VMEM((2, lay.rows * node_dev, half), BF16),
            pltpu.VMEM((out_rows, half), F32),
            pltpu.SemaphoreType.DMA((lay.rows,)),
        ],
        compiler_params=params(),
        cost_estimate=cost(4 * slots * block * block * half, 4 * lay.rows * node_dev * half),
        name="forward_product",
    )(index_own, index_other, tiles_own, tiles_other, *pieces)


def dense_and_backward(lay, sums, weight, bias, index_own, tiles_own, ups, ups_other):
    node_dev, width = ups[0].shape
    rows, half = node_dev * lay.cols, width // 2
    share = half // lay.pairs
    slots, block, _ = tiles_own.shape
    group = math.gcd(slots, 4)

    n_sums = len(sums)

    def kernel(w_ref, b_ref, idx, tiles, *refs):
        n_ups = lay.pairs + 1
        up_refs, sum_refs, refs = refs[:n_ups], refs[n_ups:][:n_sums], refs[n_ups + n_sums :]
        act_ref, gw_ref, refs = refs[0], refs[1], refs[2:]
        out_refs, (up_all, parts, hidden, gw, dh_ref, total, sems) = refs[: lay.rows], refs[lay.rows :]
        row, col = lax.axis_index("row"), lax.axis_index("col")
        pair, core = col // 2, lax.rem(col, 2)
        copies = []
        for d in range(lay.cols):
            at = pl.multiple_of(xor_to(col, d) * node_dev, node_dev)
            ref = up_refs[-1].at[d // 2] if d % 2 else up_refs[d // 2]
            copies.append(pltpu.make_async_copy(ref, up_all.at[pl.ds(at, node_dev), :], sems.at[d]))
        for n, ref in enumerate(sum_refs):
            part, dk, dx = n % 2, n // 2 % 2, n // 4
            at = pl.multiple_of(xor_to(core, dk) * half, half)
            to = parts.at[dx, pl.ds(part * (rows // 2), rows // 2), pl.ds(at, half)]
            copies.append(pltpu.make_async_copy(ref, to, sems.at[lay.cols + n]))
        ups_copies, sum_copies = copies[: lay.cols], copies[lay.cols :]
        for c in sum_copies + ups_copies:
            c.start()
        total[...] = jnp.zeros_like(total)
        for c in sum_copies:
            c.wait()
        own_half = pl.ds(pl.multiple_of(core * half, half), half)
        gb = jnp.zeros((1, width), F32)
        for j in range(lay.cols):
            sl = pl.ds(j * node_dev, node_dev)
            h = tree_sum([parts[dx, sl, :].astype(F32) for dx in range(lay.pairs)]).astype(BF16)
            hidden[sl, :] = h
            pre = jnp.dot(h, w_ref[...], preferred_element_type=F32) + b_ref[...]
            sig = jax.nn.sigmoid(pre)

            @pl.when(col == j)
            def _(pre=pre, sig=sig):
                act_ref[...] = (pre * sig).astype(BF16)

            if j == 0:
                for c in ups_copies:
                    c.wait()
            dpre = (up_all[sl, :].astype(F32) * sig * (1.0 + pre * (1.0 - sig))).astype(BF16)
            gb += jnp.sum(dpre.astype(F32), axis=0, keepdims=True)
            one = lax.dot_general(hidden[sl, own_half], dpre, (((0,), (0,)), ((), ())), preferred_element_type=F32)
            if j == 0:
                gw[...] = one
            else:
                gw[...] += one
            dh_ref[sl, :] = lax.dot_general(
                dpre, w_ref[...], (((1,), (1,)), ((), ())), preferred_element_type=F32
            ).astype(BF16)
        high = gb.astype(BF16).astype(F32)
        low = gb - high
        line = lax.broadcasted_iota(jnp.int32, (EXTRA_ROWS, width), 0)
        extra = jnp.where(line == 0, high, jnp.where(line == 1, low, 0.0)).astype(BF16)
        gw_ref[:share, :] = gw[pl.ds(pl.multiple_of(pair * share, share), share), :].astype(BF16)
        gw_ref[share:, :] = extra

        count = idx[2 * slots]

        def turn(g, carry):
            products = []
            for j in range(group):
                s = g * group + j
                at = pl.multiple_of(idx[s] * block, block)
                p = lax.dot_general(
                    tiles[s], dh_ref[pl.ds(at, block), :], (((0,), (0,)), ((), ())), preferred_element_type=F32
                )
                products.append(jnp.where(s < count, p, 0.0))
            for j, p in enumerate(products):
                to = pl.multiple_of(idx[slots + g * group + j] * block, block)
                total[pl.ds(to, block), :] += p
            return carry

        lax.fori_loop(0, (count + group - 1) // group, turn, 0)
        for d in range(lay.rows):
            at = pl.multiple_of(xor_to(row, d) * node_dev, node_dev)
            out_refs[d][...] = total[pl.ds(at, node_dev), :].astype(BF16)

    return pl.pallas_call(
        kernel,
        out_shape=[
            jax.ShapeDtypeStruct((node_dev, width), BF16),
            jax.ShapeDtypeStruct((share + EXTRA_ROWS, width), BF16),
        ]
        + [jax.ShapeDtypeStruct((node_dev, width), BF16)] * lay.rows,
        in_specs=[vmem(), vmem(), smem(), vmem()] + [hbm()] * (lay.pairs + 1 + n_sums),
        out_specs=[vmem()] * (2 + lay.rows),
        scratch_shapes=[
            pltpu.VMEM((rows, width), BF16),
            pltpu.VMEM((lay.pairs, rows, width), BF16),
            pltpu.VMEM((rows, width), BF16),
            pltpu.VMEM((half, width), F32),
            pltpu.VMEM((rows, width), BF16),
            pltpu.VMEM((lay.rows * node_dev, width), F32),
            pltpu.SemaphoreType.DMA((lay.cols + n_sums,)),
        ],
        compiler_params=params(),
        cost_estimate=cost(5 * rows * width * width, 8 * rows * width),
        name="dense_and_backward",
    )(weight, bias, index_own, tiles_own, *ups, ups_other, *sums)


def place_weight_gradient(lay, own, other, width):
    half = width // 2
    share = half // lay.pairs

    def kernel(*refs):
        own_refs, other_refs, out_ref = refs[: lay.pairs], refs[lay.pairs : 2 * lay.pairs], refs[-1]
        col = lax.axis_index("col")
        pair, core = col // 2, lax.rem(col, 2)
        for dk, shares in enumerate((own_refs, other_refs)):
            for dx in range(lay.pairs):
                at = pl.multiple_of(xor_to(core, dk) * half + xor_to(pair, dx) * share, share)
                out_ref[pl.ds(at, share), :] = shares[dx][...].astype(F32)

    return pl.pallas_call(
        kernel,
        out_shape=jax.ShapeDtypeStruct((width, width), F32),
        in_specs=[vmem()] * (2 * lay.pairs),
        out_specs=vmem(),
        compiler_params=params(),
        cost_estimate=cost(width * width, 6 * width * width),
        name="place_weight_gradient",
    )(*own, *other)


def split_bias(total, width):
    line_sum = total[-EXTRA_ROWS] + total[1 - EXTRA_ROWS]
    high = line_sum.astype(BF16)
    low = (line_sum - high.astype(F32)).astype(BF16)
    line = jnp.arange(EXTRA_ROWS)[:, None]
    extra = jnp.where(line == 0, high[None], jnp.where(line == 1, low[None], jnp.zeros((), BF16)))
    return jnp.concatenate([total[:-EXTRA_ROWS].astype(BF16), extra])


def shards(features, blocks, block_rows, block_cols, block_count, weight, bias_vector, upstream):
    lay = Layout(lax.axis_size("row"), lax.axis_size("col"))
    node_dev, width = features.shape
    half = width // 2
    scale = 1.0 / math.sqrt(node_dev * lay.rows * lay.cols)
    tiles = blocks[0, 0]
    core = lax.axis_index("col") % 2

    mine = [jnp.where(core == 0, a[:, :half], a[:, half:]) for a in (features, lay.move_col(features, core=1))]
    piece = jnp.stack(mine)

    piece, upstream = lax.optimization_barrier((piece, upstream))
    gathered = {0: piece}

    def over_fast(dz):
        for dy in range(1, lay.fast):
            gathered[dz * lay.fast + dy] = lay.move_row(gathered[dz * lay.fast], fast=dy)

    def over_fast_of(dz):
        return [gathered[dz * lay.fast + dy] for dy in range(1, lay.fast)]

    for dz in reversed(range(1, lay.slow)):
        if dz & (dz - 1) == 0:
            gathered[dz * lay.fast] = lay.move_row(piece, slow=dz)
    over_fast(0)
    ups = [upstream] + [lay.move_col(upstream, pair=dx) for dx in range(1, lay.pairs)]
    one = lay.fast if lay.slow > 1 else 0
    near, gathered[one], later = lax.optimization_barrier(
        (over_fast_of(0), gathered[one], (block_rows, block_cols, block_count, tiles))
    )
    block_rows, block_cols, block_count, tiles = later
    index = jnp.concatenate([block_rows[0, 0], block_cols[0, 0], block_count[0]])
    gathered.update(zip(range(1, lay.fast), near))
    index_other = lay.move_col(index, core=1)
    tiles_other = lay.move_col(tiles, core=1)
    ups_other = lay.move_col(jnp.stack(ups), core=1)
    for dz in range(1, lay.slow):
        top = 1 << (dz.bit_length() - 1)
        if dz != top:
            gathered[dz * lay.fast] = lay.move_row(gathered[top * lay.fast], slow=dz ^ top)
    others = (index_other, tiles_other, ups_other)
    for dz in range(1, lay.slow):
        over_fast(dz)
        if dz < lay.slow - 1:
            after = (dz + 1) * lay.fast
            extra = others if dz == lay.slow - 2 else ()
            gathered[after], done, extra = lax.optimization_barrier((gathered[after], over_fast_of(dz), extra))
            gathered.update(zip(range(dz * lay.fast + 1, after), done))
            others = extra or others
    index_other, tiles_other, ups_other = others
    pieces = [gathered[d] for d in range(lay.rows)]

    mine = forward_product(lay, index, index_other, tiles, tiles_other, pieces, node_dev * lay.cols)
    sums = list(mine) + [lay.move_col(a, core=1) for a in mine]
    for dx in range(1, lay.pairs):
        came = [lay.move_col(a, pair=dx) for a in mine]
        sums += came + [lay.move_col(a, core=1) for a in came]

    activated, gw, *outs = dense_and_backward(
        lay, sums, weight, bias_vector[None], index, tiles, ups, ups_other
    )

    def fast_arrivals(dz):
        return [lay.move_row(outs[dz * lay.fast + dy], fast=dy) for dy in range(1, lay.fast)]

    def fast_sum(dz, arrived):
        return sum([a.astype(F32) for a in arrived], outs[dz * lay.fast].astype(F32))

    def hold(dz, until):
        span = slice(dz * lay.fast + 1, (dz + 1) * lay.fast)
        until, outs[span] = lax.optimization_barrier((until, outs[span]))
        return until

    def slow_sum(dz):
        top = 1 << (dz.bit_length() - 1)
        to, hop = (top, dz ^ top) if dz != top else (0, dz)
        sums[to] = sums[to] + lay.move_row(sums[dz].astype(BF16), slow=hop).astype(F32)

    hops = [dict(slow=1 << i) for i in range(lay.slow.bit_length() - 1)]
    hops += [dict(fast=1 << i) for i in range(lay.fast.bit_length() - 1)]
    sums = {}
    if lay.slow > 2:
        sums[3] = hold(2, fast_sum(3, fast_arrivals(3)).astype(BF16))
        sums[2] = fast_sum(2, fast_arrivals(2))
        slow_sum(3)
    came = None
    for n, hop in enumerate(hops):
        if n:
            gw = split_bias(gw.astype(F32) + came.astype(F32), width)
            if hop.get("fast") == 1 and lay.slow > 2:
                gw = hold(1, gw)
                gw, sums[2] = lax.optimization_barrier((gw, sums[2]))
        came = lay.move_row(gw, **hop)
    came = hold(0, came)
    for dz in range(min(2, lay.slow)):
        sums[dz] = fast_sum(dz, fast_arrivals(dz))
    for dz in reversed(range(1, min(3, lay.slow))):
        slow_sum(dz)
    grad_features = sums[0].astype(BF16)

    total = (gw.astype(F32) + came.astype(F32)) * scale
    grad_bias = total[-EXTRA_ROWS] + total[1 - EXTRA_ROWS]
    share = total[:-EXTRA_ROWS].astype(BF16)
    own = [share] + [lay.move_col(share, pair=dx) for dx in range(1, lay.pairs)]
    other = lay.move_col(jnp.stack(own), core=1)
    grad_weight = place_weight_gradient(lay, own, [other[i] for i in range(lay.pairs)], width)
    return (activated, grad_weight, grad_bias, grad_features)


def solution(mesh):
    in_specs = (
        P(("col", "row"), None),
        P("row", "col", None, None, None),
        P("row", "col", None),
        P("row", "col", None),
        P("row", "col"),
        P(),
        P(),
        P(("row", "col"), None),
    )
    out_specs = (P(("row", "col"), None), P(), P(), P(("col", "row"), None))
    return jax.shard_map(shards, mesh=mesh, in_specs=in_specs, out_specs=out_specs, check_vma=False)
```
